512 devices in a mesh: rep: 4 (over z_lo), row: 128 (over y, z_hi, x, core).
Axes of the slice: x: 4, y: 8, z: 8 (z_hi: 2, z_lo: 4; z = z_hi * 4 + z_lo), core: 2. Of those that a mesh axis runs over, the one named last changes fastest.
Arguments:
- features: bfloat16 [65536, 128], P(('rep', 'row')), may hold values from -6 to 6
- node_order: int32 [512, 128], P(('rep', 'row')), may hold values from 0 to 127, each once within a row
- tile_values: bfloat16 [4, 128, 135, 128, 128], P('rep', 'row'), as said below
- tile_row: int32 [4, 128, 135], P('rep', 'row'), may hold values from 0 to 3, as said below
- tile_col: int32 [4, 128, 135], P('rep', 'row'), may hold values from 0 to 127
- tile_count: int32 [4, 128], P('rep', 'row'), may hold values from 1 to 135, as said below
- weight: bfloat16 [128, 256], replicated, may hold values from -0.5 to 0.5
- bias_vec: float32 [256], replicated, may hold values from -3 to 3
- cotangent: bfloat16 [65536, 256], P(('rep', 'row')), may hold values from -6 to 6
Outputs:
- activations: bfloat16 [65536, 256], P(('rep', 'row'))
- feature_grad: float32 [65536, 128], P(('rep', 'row'))
- weight_grad: float32 [128, 256], replicated
- bias_grad: float32 [256], replicated
The draws below stay inside these ranges and needn't reach their ends.
Inputs may be any that keep to these rules, and one draw needn't show every extreme that they name: Slots 0 to tile_count - 1 of a device hold its tiles, later slots hold arbitrary values; some device uses all 135 slots in every draw. Within a device's used slots the pairs (tile_row, tile_col) are distinct. A is symmetric: the tile at block (g, h) is the transpose of the tile at block (h, g). `tile_values`: tiles at used slots assemble the symmetric matrix A.
All inputs are finite; a program needn't handle non-finite values.
Results may differ from the reference program's by a relative error of at most 0.015.
Values may be sent and summed in bfloat16 or wider, within the bound.
A program may use at most 64 MiB of HBM per device.

```python
import jax
import jax.numpy as jnp
from jax import lax

TILE = 128
F = 128
HID = 256
BLOCKS = 512
NODES = 65536
SLOTS = 135
N_REP = 4
N_ROW = 128


def layout(key):
    blocks = N_ROW * N_REP
    half_len = (SLOTS - 1) // 2
    target = N_ROW // 2
    shuffled = (jax.random.permutation(jax.random.fold_in(key, 11), blocks // 2 - 1) + 1).astype(jnp.int32)
    places = jnp.arange(blocks // 2 - 1, dtype=jnp.int32)
    ordering = jnp.argsort(jnp.where(shuffled == target, -1, places))
    ordered = shuffled[ordering]
    chosen = ordered[:half_len].astype(jnp.int32)
    offsets = jnp.concatenate([jnp.zeros((1,), jnp.int32), chosen, blocks - chosen])
    density = jax.random.randint(jax.random.fold_in(key, 12), (blocks,), 20, 101)
    full_rep = jax.random.randint(jax.random.fold_in(key, 13), (), 0, N_REP)
    full_row = jax.random.randint(jax.random.fold_in(key, 14), (), 0, N_ROW)
    rep_ids = jnp.arange(N_REP, dtype=jnp.int32)[:, None, None]
    row_ids = jnp.arange(N_ROW, dtype=jnp.int32)[None, :, None]
    shifts = offsets[None, None, :]
    col_local = (row_ids + shifts) % N_ROW
    col_block = rep_ids * N_ROW + col_local
    row_block = (col_block - shifts) % blocks
    row_block = jnp.broadcast_to(row_block, (N_REP, N_ROW, SLOTS))
    col_block = jnp.broadcast_to(col_block, (N_REP, N_ROW, SLOTS))
    lower = jnp.minimum(row_block, col_block)
    upper = jnp.maximum(row_block, col_block)
    pair_ids = (lower * blocks + upper).reshape(-1)
    pair_key = jax.random.fold_in(key, 15)
    chance = jax.vmap(lambda pair: jax.random.randint(jax.random.fold_in(pair_key, pair), (), 0, 100))(pair_ids)
    chance = chance.reshape(N_REP, N_ROW, SLOTS)
    forced = (row_block % N_ROW == full_row) & (col_block // N_ROW == full_rep) | (col_block % N_ROW == full_row) & (row_block // N_ROW == full_rep)
    across = jnp.broadcast_to((shifts == target) | (shifts == blocks - target), (N_REP, N_ROW, SLOTS))
    keep = (row_block == col_block) | forced | across | (chance < jnp.minimum(density[row_block], density[col_block]))
    scores = (1 - keep.astype(jnp.int32)) * SLOTS + jnp.arange(SLOTS, dtype=jnp.int32)
    ranking = jnp.argsort(scores, axis=-1)
    row_sorted = jnp.take_along_axis(row_block, ranking, axis=-1)
    col_sorted = jnp.take_along_axis(col_block, ranking, axis=-1)
    counts = jnp.sum(keep.astype(jnp.int32), axis=-1)
    return (row_sorted, col_sorted, counts)


def draw_tile_row(key, part):
    row_sorted, col_sorted, counts = layout(key)
    return (row_sorted // N_ROW).astype(jnp.int32)


def draw_tile_col(key, part):
    row_sorted, col_sorted, counts = layout(key)
    return (col_sorted % N_ROW).astype(jnp.int32)


def draw_tile_count(key, part):
    row_sorted, col_sorted, counts = layout(key)
    return counts.astype(jnp.int32)


def draw_tile_values(key, part):
    row_sorted, col_sorted, counts = layout(key)
    key = jax.random.fold_in(key, 5)
    blocks = N_ROW * N_REP
    scale = (TILE * SLOTS * 0.5) ** (-0.5)

    def one_tile(row_block, col_block):
        lower = jnp.minimum(row_block, col_block)
        upper = jnp.maximum(row_block, col_block)
        tile_key = jax.random.fold_in(key, lower * blocks + upper)
        base = jax.random.normal(tile_key, (TILE, TILE), jnp.float32)
        placed = jnp.where(row_block < col_block, base, base.T)
        placed = jnp.where(row_block == col_block, (base + base.T) * 0.70710678, placed)
        return (placed * scale).astype(jnp.bfloat16)
    flat_rows = row_sorted.reshape(-1, SLOTS)
    flat_cols = col_sorted.reshape(-1, SLOTS)
    drawn = lax.map(lambda pair: jax.vmap(one_tile)(pair[0], pair[1]), (flat_rows, flat_cols))
    return drawn.reshape(N_REP, N_ROW, SLOTS, TILE, TILE)


def level_of(key, dims, pieces, least, high):
    loudness, own = 1.0, jax.random.fold_in(key, 6)
    for position, parts in pieces:
        draws = jnp.exp(jax.random.uniform(jax.random.fold_in(own, position), (parts,), jnp.float32, least / len(pieces), high / len(pieces)))
        loudness = loudness * jnp.repeat(draws, dims[position] // parts).reshape([-1 if axis == position else 1 for axis in range(len(dims))])
    return loudness


def bell_draw(own_key, shape, spread, reach, split=(), held_as=jnp.bfloat16):
    gain = level_of(own_key, shape, split, -0.22, 0.18) if split else 1.0
    array = jax.random.normal(own_key, shape, jnp.float32) * spread * gain
    return jnp.minimum(jnp.maximum(array, -reach), reach).astype(held_as)


def setup_inputs(seed: int = 0) -> dict:
    seeds = jax.random.split(jax.random.key(seed), 10)
    return {
        "features": bell_draw(seeds[0], (NODES, F), 1.0, 6.0, ((0, 512),)),
        "node_order": jax.vmap(lambda own: jax.random.permutation(own, TILE))(jax.random.split(seeds[1], BLOCKS)).reshape((BLOCKS, TILE)).astype(jnp.int32),
        "tile_values": draw_tile_values(jax.random.fold_in(seeds[9], 71), 0),
        "tile_row": draw_tile_row(jax.random.fold_in(seeds[9], 71), 0),
        "tile_col": draw_tile_col(jax.random.fold_in(seeds[9], 71), 0),
        "tile_count": draw_tile_count(jax.random.fold_in(seeds[9], 71), 0),
        "weight": bell_draw(seeds[6], (F, HID), F ** -0.5, 0.5),
        "bias_vec": bell_draw(seeds[7], (HID,), 0.5, 3.0, (), jnp.float32),
        "cotangent": bell_draw(seeds[8], (NODES, HID), 1.0, 6.0, ((0, 512),)),
    }


def aggregate(values, tile_values, tile_row, tile_col, tile_count):
    feat_len = values.shape[-1]
    blocks = values.reshape(N_REP * N_ROW, TILE, feat_len)
    slot_ids = jnp.arange(SLOTS, dtype=jnp.int32)
    rep_ids = jnp.arange(N_REP, dtype=jnp.int32)

    def one_device(replica, row_index):
        mats = tile_values[replica, row_index].astype(jnp.float32)
        picked = blocks[replica * N_ROW + tile_col[replica, row_index]].astype(jnp.float32)
        products = jnp.einsum('kab,kbw->kaw', mats, picked)
        chosen = (tile_row[replica, row_index][None, :] == rep_ids[:, None]) & (slot_ids[None, :] < tile_count[replica, row_index])
        return jnp.einsum('ik,kaw->iaw', chosen.astype(jnp.float32), products)

    def one_row(row_index):
        return jnp.sum(jax.vmap(lambda replica: one_device(replica, row_index))(rep_ids), axis=0)

    summed = lax.map(one_row, jnp.arange(N_ROW, dtype=jnp.int32))
    return jnp.transpose(summed, (1, 0, 2, 3)).reshape(N_REP * N_ROW * TILE, feat_len)


def reference(features, node_order, tile_values, tile_row, tile_col, tile_count, weight, bias_vec, cotangent):
    places = (jnp.arange(N_REP * N_ROW, dtype=jnp.int32)[:, None] * TILE + node_order).reshape(-1)
    permuted = features[places]
    hidden = aggregate(permuted, tile_values, tile_row, tile_col, tile_count).astype(jnp.bfloat16)
    pre_act = jnp.dot(hidden, weight, preferred_element_type=jnp.float32) + bias_vec
    activations = jax.nn.silu(pre_act).astype(jnp.bfloat16)
    sigmoid_pre = jax.nn.sigmoid(pre_act)
    pre_grad = (cotangent.astype(jnp.float32) * sigmoid_pre * (1.0 + pre_act * (1.0 - sigmoid_pre))).astype(jnp.bfloat16)
    weight_grad = jnp.dot(hidden.T, pre_grad, preferred_element_type=jnp.float32)
    bias_grad = jnp.sum(pre_grad.astype(jnp.float32), axis=0)
    hidden_grad = jnp.dot(pre_grad, weight.T, preferred_element_type=jnp.float32).astype(jnp.bfloat16)
    permuted_grad = aggregate(hidden_grad, tile_values, tile_row, tile_col, tile_count)
    feature_grad = jnp.zeros((N_REP * N_ROW * TILE, F), jnp.float32).at[places].set(permuted_grad)
    return activations, feature_grad, weight_grad, bias_grad
```

```python
import functools

import jax
import jax.numpy as jnp
from jax import lax
from jax.experimental import pallas as pl
from jax.experimental.pallas import tpu as pltpu
from jax.sharding import PartitionSpec as P

MESH = pl.DeviceIdType.MESH
NX, NY, NZ = 4, 8, 8
T = 128
R1, R2 = 64, 64
SLOTS = 135
DELTAS = (0, -1, 1, -2, 2, -3, 3, 4)
XIS = (0, -1, 1, 2)
GROUPS = ((0, 1), (1, 2), (3, 2), (5, 3))
ROWS = 64 * (R1 + R2)


def row1(ab, d, xi):
    return ((ab * 8 + d) * 4 + xi) * R1


def row2(ab, xi, d):
    return 64 * R1 + ((ab * 4 + xi) * 8 + d) * R2


def sem_x1(ab):
    return ab


SEM_Z = 2


def sem_y1(ab, d):
    return 3 + ab * 7 + d - 1


def sem_y2(ab, d):
    return 17 + ab * 7 + d - 1


def sem_x2(ab, xi, g):
    return 31 + (ab * 3 + xi - 1) * 4 + g


def sem_sib(ab, g):
    return 55 + ab * 4 + g


N_RECV = 63
SEND_Z, SEND_X1, SEND_Y1, SEND_Y2, SEND_X2, SEND_SIB = range(6)


def kernel(
    features, order, tiles_hbm, table, weight, bias, cotangent,
    act_out, fgrad_out, wgrad_out, bgrad_out,
    tiles, G, acc, part, part_in, wp, wp_in, w2, w2_in, w3, w3_in, wq, wfull,
    tile_sem, recv, send, rs_recv, rs_send, ar_recv, ar_send,
):
    q = lax.axis_index("rep")
    r = lax.axis_index("row")
    y, zh, x, c = r // 16, (r // 8) % 2, (r // 2) % 4, r % 2
    z = zh * 4 + q

    def dev(dy=0, dx=0, dc=0):
        ny, nx, nc = (y + dy) % NY, (x + dx) % NX, (c + dc) % 2
        return (q, ny * 16 + zh * 8 + nx * 2 + nc)

    def dev_z(dz):
        nz = (z + dz) % NZ
        return (nz % 4, y * 16 + (nz // 4) * 8 + x * 2 + c)

    def dev_rep(dq):
        return ((q + dq) % 4, r)

    z_partner = dev_z(4)
    right_y, left_y, right_x, left_x = dev(dy=1), dev(dy=NY - 1), dev(dx=1), dev(dx=NX - 1)
    sibling = dev(dc=1)
    line_y = [dev(dy=j) for j in range(1, NY)]
    line_xc = [(dx, dc, dev(dx=dx, dc=dc)) for dx in range(NX) for dc in range(2) if dx or dc]
    line_z = [dev_z(j) for j in range(1, NZ)]

    barrier = pltpu.get_barrier_semaphore()
    for peer in line_y + [p for _, _, p in line_xc] + line_z:
        pl.semaphore_signal(barrier, inc=1, device_id=peer, device_id_type=MESH)

    load = pltpu.make_async_copy(tiles_hbm, tiles.at[pl.ds(0, SLOTS)], tile_sem)
    load.start()
    tiles[SLOTS] = jnp.zeros((T, T), jnp.bfloat16)

    places = lax.broadcasted_iota(jnp.int32, (T, T), 0) == order[...]
    onehot = places.astype(jnp.float32).astype(jnp.bfloat16)

    def store_own(p, block):
        G[p, 0, pl.ds(row1(0, 0, 0), R1)] = block[:R1]
        G[p, 0, pl.ds(row2(0, 0, 0), R2)] = block[R1:]

    store_own(0, lax.dot_general(
        onehot, features[...], (((0,), (0,)), ((), ())), preferred_element_type=jnp.float32
    ).astype(jnp.bfloat16))
    acc[...] = jnp.zeros_like(acc)

    pl.semaphore_wait(barrier, 21)

    def push(src, dst, send_sem, recv_sem, device):
        pltpu.make_async_remote_copy(
            src_ref=src, dst_ref=dst, send_sem=send_sem, recv_sem=recv_sem,
            device_id=device, device_id_type=MESH,
        ).start()

    def await_ref(ref, sem):
        pltpu.make_async_copy(ref, ref, sem).wait()

    def steps(p):
        own = G.at[p, 0]
        other = G.at[p, 1]

        def go(src, dst, n, kind, sem, device):
            push(own.at[pl.ds(src, n)], own.at[pl.ds(dst, n)], send.at[p, kind], recv.at[p, sem], device)

        def wait(sem, n):
            await_ref(own.at[pl.ds(0, n)], recv.at[p, sem])

        def sib(at, n, ab, g):
            push(own.at[pl.ds(at, n)], other.at[pl.ds(at, n)], send.at[p, SEND_SIB], recv.at[p, sem_sib(ab, g)], sibling)

        def sib1(ab, d):
            sib(row1(ab, d, 0), 4 * R1, ab, (0, 1, 1, 2, 2, 3, 3, 3)[d])

        def sib2(ab, xi, g):
            sib(row2(ab, xi, GROUPS[g][0]), GROUPS[g][1] * R2, ab, g)

        def send_x1(ab):
            for dx, xi in ((1, 1), (3, 2), (2, 3)):
                go(row1(ab, 0, 0), row1(ab, 0, xi), R1, SEND_X1, sem_x1(ab), dev(dx=dx))

        def y1(ab, src, dst, device):
            go(row1(ab, src, 0), row1(ab, dst, 0), 4 * R1, SEND_Y1, sem_y1(ab, dst), device)

        def y2(ab, src, dst, device):
            go(row2(ab, 0, src), row2(ab, 0, dst), R2, SEND_Y2, sem_y2(ab, dst), device)

        def x2(ab, src, dst, g, device):
            d, n = GROUPS[g]
            go(row2(ab, src, d), row2(ab, dst, d), n * R2, SEND_X2, sem_x2(ab, dst, g), device)

        def x2_own(ab, g):
            x2(ab, 0, 1, g, right_x)
            x2(ab, 0, 2, g, left_x)
            sib2(ab, 0, g)

        def x2_pass(ab, g):
            n = GROUPS[g][1] * R2
            wait(sem_x2(ab, 1, g), n)
            if g in (0, 3):
                x2(ab, 1, 3, g, right_x)
            wait(sem_x2(ab, 2, g), n)
            if g in (1, 2):
                x2(ab, 2, 3, g, left_x)
            sib2(ab, 1, g)
            sib2(ab, 2, g)

        def x2_last(ab, g):
            wait(sem_x2(ab, 3, g), GROUPS[g][1] * R2)
            sib2(ab, 3, g)

        def ring_pass(ab, hop, sem, move, n, after):
            lo, hi = 2 * hop - 1, 2 * hop
            wait(sem(ab, lo), n)
            if hop < 3:
                move(ab, lo, lo + 2, right_y)
            elif ab == 0:
                move(ab, lo, 7, right_y)
            wait(sem(ab, hi), n)
            if hop < 3:
                move(ab, hi, hi + 2, left_y)
            elif ab == 1:
                move(ab, hi, 7, left_y)
            if after:
                sib1(ab, lo)
                sib1(ab, hi)

        def y1_pass(ab, hop):
            ring_pass(ab, hop, sem_y1, y1, 4 * R1, True)

        def y2_pass(ab, hop):
            ring_pass(ab, hop, sem_y2, y2, R2, False)

        def compute(ab, g):
            d0, n = GROUPS[g]
            await_ref(other.at[pl.ds(0, n * 512)], recv.at[p, sem_sib(ab, g)])

            def body(i, carry):
                d, k = d0 + i // 2, i % 2
                base = (ab * 8 + d) * 32 + k * 4
                left = jnp.concatenate([
                    jnp.concatenate([tiles[table[base + xi * 8 + j]] for xi in range(4)], axis=1)
                    for j in range(4)
                ], axis=0)
                pieces = []
                for xi in range(4):
                    pieces.append(G[p, k, pl.ds(pl.multiple_of(row1(ab, d, xi), R1), R1)])
                    pieces.append(G[p, k, pl.ds(pl.multiple_of(row2(ab, xi, d), R2), R2)])
                right = jnp.concatenate(pieces, axis=0)
                acc[...] += jnp.dot(left, right, preferred_element_type=jnp.float32)
                return carry

            lax.fori_loop(0, 2 * n, body, 0)

        def s0(ab):
            if ab == 1:
                wait(SEM_Z, R1 + R2)
            send_x1(ab)
            y2(ab, 0, 1, right_y)
            y2(ab, 0, 2, left_y)
            if ab == 0:
                for at, n in ((row1(0, 0, 0), R1), (row2(0, 0, 0), R2)):
                    dst = row1(1, 0, 0) if n == R1 and at == row1(0, 0, 0) else row2(1, 0, 0)
                    go(at, dst, n, SEND_Z, SEM_Z, z_partner)
            x2_own(ab, 0)

        def s1(ab):
            wait(sem_x1(ab), 3 * R1)
            y1(ab, 0, 1, right_y)
            y1(ab, 0, 2, left_y)
            sib1(ab, 0)

        def s2(ab):
            y2_pass(ab, 1)
            x2_own(ab, 1)

        def s3(ab):
            x2_pass(ab, 0)

        def s4(ab):
            y2_pass(ab, 2)
            x2_own(ab, 2)

        def s5(ab):
            y1_pass(ab, 1)

        def s6(ab):
            x2_pass(ab, 1)

        def s7(ab):
            y2_pass(ab, 3)

        def s8(ab):
            wait(sem_y2(ab, 7), R2)
            x2_own(ab, 3)

        def s9(ab):
            x2_last(ab, 0)

        def s10(ab):
            y1_pass(ab, 2)

        def s11(ab):
            x2_pass(ab, 2)

        def s12(ab):
            x2_last(ab, 1)

        def s13(ab):
            y1_pass(ab, 3)

        def s14(ab):
            x2_pass(ab, 3)

        def s15(ab):
            x2_last(ab, 2)

        def s16(ab):
            wait(sem_y1(ab, 7), 4 * R1)
            sib1(ab, 7)

        def s17(ab):
            x2_last(ab, 3)

        def finish():
            for kind, n in ((SEND_Z, R1 + R2), (SEND_X1, 6 * R1), (SEND_Y1, 56 * R1), (SEND_Y2, 14 * R2), (SEND_X2, 48 * R2), (SEND_SIB, ROWS)):
                await_ref(own.at[pl.ds(0, n)], send.at[p, kind])

        table_of = {f"s{i}": f for i, f in enumerate(
            (s0, s1, s2, s3, s4, s5, s6, s7, s8, s9, s10, s11, s12, s13, s14, s15, s16, s17))}
        for g in range(4):
            table_of[f"c{g}"] = functools.partial(lambda g, ab: compute(ab, g), g)
        return table_of, finish

    PLAN = (
        "a s0 s1 s2 s3 b s0 a s4 s5 b s1 a s6 s7 b s2 a s8 s9 c0 b s3 a s10 b s4 a s11 s12 c1 b s5 a s13 b s6 s7"
        " a s14 s15 c2 b s8 s9 c0 a s16 s17 c3 b s10 s11 s12 c1 s13 s14 s15 c2 s16 s17 c3"
    ).split()

    def run(p, extra):
        table_of, finish = steps(p)
        ab = 0
        for at, word in enumerate(PLAN):
            if word in ("a", "b"):
                ab = "ab".index(word)
                continue
            table_of[word](ab)
            for f in extra.get(("ab"[ab], word), ()):
                f()
        return finish

    def reduce_rep(p):
        for j in range(1, 4):
            part[p, j - 1] = acc[pl.ds(j * T, T)].astype(jnp.bfloat16)
        for j in range(1, 4):
            push(part.at[p, j - 1], part_in.at[p, j - 1], rs_send.at[p], rs_recv.at[p], dev_rep(j))
        await_ref(part_in.at[p], rs_recv.at[p])
        total = acc[pl.ds(0, T)]
        for j in range(3):
            total = total + part_in[p, j].astype(jnp.float32)
        return total

    finish0 = run(0, {("a", "s3"): (load.wait,)})
    hidden = reduce_rep(0).astype(jnp.bfloat16)
    pre_act = jnp.dot(hidden, weight[...], preferred_element_type=jnp.float32) + bias[...]
    gate = jax.nn.sigmoid(pre_act)
    pre_grad = (cotangent[...].astype(jnp.float32) * gate * (1.0 + pre_act * (1.0 - gate))).astype(jnp.bfloat16)
    store_own(1, lax.dot_general(
        pre_grad, weight[...], (((1,), (1,)), ((), ())), preferred_element_type=jnp.float32
    ).astype(jnp.bfloat16))
    acc[...] = jnp.zeros_like(acc)

    def terms():
        act_out[...] = (pre_act * gate).astype(jnp.bfloat16)
        weight_term = lax.dot_general(
            hidden, pre_grad, (((0,), (0,)), ((), ())), preferred_element_type=jnp.float32
        )
        bias_term = jnp.sum(pre_grad.astype(jnp.float32), axis=0, keepdims=True)
        rows = lax.broadcasted_iota(jnp.int32, (8, T), 0)
        bias_tile = jnp.where(rows == 0, bias_term[:, :T], jnp.where(rows == 1, bias_term[:, T:], 0.0))
        for piece in range(NZ):
            for t in range(4):
                wp[piece, t] = weight_term[piece * 16 + (t // 2) * 8:piece * 16 + (t // 2) * 8 + 8, (t % 2) * T:(t % 2) * T + T]
            wp[piece, 4] = bias_tile

    def ar1():
        for j in range(1, NZ):
            push(wp.at[(z + j) % NZ], wp_in.at[j - 1], ar_send.at[0], ar_recv.at[0], dev_z(j))

    def ar2():
        await_ref(wp_in, ar_recv.at[0])
        total = wp[z]
        for j in range(NZ - 1):
            total = total + wp_in[j]
        for t in range(4):
            w2[t, 0] = total[t]
            w2[t, 1] = total[4]
        for dx, dc, device in line_xc:
            push(w2.at[(x + dx) % NX], w2_in.at[((NX - dx) % NX) * 2 + dc - 1], ar_send.at[1], ar_recv.at[1], device)

    def ar3():
        await_ref(w2_in, ar_recv.at[1])
        total = w2[x]
        for j in range(7):
            total = total + w2_in[j]
        w3[...] = total
        for j in range(1, NY):
            push(w3, w3_in.at[j - 1], ar_send.at[2], ar_recv.at[2], dev(dy=j))

    def ar4():
        await_ref(w3_in, ar_recv.at[2])
        total = w3[...]
        for j in range(NY - 1):
            total = total + w3_in[j]
        bgrad_out[...] = total[1]
        wq[x] = total[0]
        for dx in range(1, NX):
            push(wq.at[x], wq.at[x], ar_send.at[3], ar_recv.at[3], dev(dx=dx))

    def ar5():
        await_ref(wq.at[pl.ds(0, NX - 1)], ar_recv.at[3])
        wfull[z] = wq[...]
        for j in range(1, NZ):
            push(wfull.at[z], wfull.at[z], ar_send.at[4], ar_recv.at[4], dev_z(j))

    finish1 = run(1, {
        ("a", "s0"): (terms,), ("b", "s2"): (ar1,), ("b", "s4"): (ar2,), ("b", "s7"): (ar3,), ("a", "c3"): (ar4,), ("b", "s12"): (ar5,),
    })
    total = reduce_rep(1)
    grad = None
    for _ in range(3):
        piece = total.astype(jnp.bfloat16)
        total = total - piece.astype(jnp.float32)
        moved = jnp.dot(onehot, piece, preferred_element_type=jnp.float32)
        grad = moved if grad is None else grad + moved
    fgrad_out[...] = grad

    await_ref(wfull.at[pl.ds(0, NZ - 1)], ar_recv.at[4])
    for piece in range(NZ):
        for t in range(4):
            wgrad_out[pl.ds(piece * 16 + (t // 2) * 8, 8), pl.ds((t % 2) * T, T)] = wfull[piece, t]

    finish0()
    finish1()
    for p in range(2):
        await_ref(part.at[p], rs_send.at[p])
    await_ref(wp.at[pl.ds(0, NZ - 1)], ar_send.at[0])
    await_ref(w2_in, ar_send.at[1])
    await_ref(w3_in, ar_send.at[2])
    await_ref(wq.at[pl.ds(0, NX - 1)], ar_send.at[3])
    await_ref(wfull.at[pl.ds(0, NZ - 1)], ar_send.at[4])


def slot_table(tile_row, tile_col, tile_count):
    q = lax.axis_index("rep")
    r = lax.axis_index("row")
    y, zh, x, c = r // 16, (r // 8) % 2, (r // 2) % 4, r % 2
    place = jnp.arange(512, dtype=jnp.int32)
    j, k, xi, d, ab = place % 4, (place // 4) % 2, (place // 8) % 4, (place // 32) % 8, place // 256
    dy = jnp.where(d == 7, 4, jnp.where(d % 2 == 1, -((d + 1) // 2), d // 2))
    dx = jnp.where(xi == 3, 2, jnp.where(xi == 1, -1, xi // 2))
    col = ((y + dy) % NY) * 16 + (zh + ab) % 2 * 8 + ((x + dx) % NX) * 2 + (c + k) % 2
    want = col * 4 + (q + j) % 4
    have = tile_col.reshape(SLOTS) * 4 + tile_row.reshape(SLOTS)
    slots = jnp.arange(SLOTS, dtype=jnp.int32)
    hit = (want[:, None] == have[None, :]) & (slots[None, :] < tile_count.reshape(1, 1))
    return jnp.min(jnp.where(hit, slots[None, :], SLOTS), axis=1)


def local(
    features, node_order, tile_values, tile_row, tile_col, tile_count, weight, bias_vec, cotangent
):
    table = slot_table(tile_row, tile_col, tile_count)
    vmem = pl.BlockSpec(memory_space=pltpu.VMEM)
    act, fgrad, wgrad, bgrad = pl.pallas_call(
        kernel,
        out_shape=(
            jax.ShapeDtypeStruct((T, 256), jnp.bfloat16),
            jax.ShapeDtypeStruct((T, T), jnp.float32),
            jax.ShapeDtypeStruct((T, 256), jnp.float32),
            jax.ShapeDtypeStruct((8, T), jnp.float32),
        ),
        in_specs=[
            vmem, vmem, pl.BlockSpec(memory_space=pl.ANY), pl.BlockSpec(memory_space=pltpu.SMEM), vmem, vmem, vmem,
        ],
        out_specs=(vmem, vmem, vmem, vmem),
        scratch_shapes=[
            pltpu.VMEM((SLOTS + 1, T, T), jnp.bfloat16),
            pltpu.VMEM((2, 2, ROWS, T), jnp.bfloat16),
            pltpu.VMEM((4 * T, T), jnp.float32),
            pltpu.VMEM((2, 3, T, T), jnp.bfloat16),
            pltpu.VMEM((2, 3, T, T), jnp.bfloat16),
            pltpu.VMEM((NZ, 5, 8, T), jnp.float32),
            pltpu.VMEM((NZ - 1, 5, 8, T), jnp.float32),
            pltpu.VMEM((NX, 2, 8, T), jnp.float32),
            pltpu.VMEM((7, 2, 8, T), jnp.float32),
            pltpu.VMEM((2, 8, T), jnp.float32),
            pltpu.VMEM((NY - 1, 2, 8, T), jnp.float32),
            pltpu.VMEM((NX, 8, T), jnp.float32),
            pltpu.VMEM((NZ, 4, 8, T), jnp.float32),
            pltpu.SemaphoreType.DMA,
            pltpu.SemaphoreType.DMA((2, N_RECV)),
            pltpu.SemaphoreType.DMA((2, 6)),
            pltpu.SemaphoreType.DMA((2,)),
            pltpu.SemaphoreType.DMA((2,)),
            pltpu.SemaphoreType.DMA((5,)),
            pltpu.SemaphoreType.DMA((5,)),
        ],
        compiler_params=pltpu.CompilerParams(
            collective_id=0, has_side_effects=True, vmem_limit_bytes=48 * 1024 * 1024
        ),
    )(
        features, node_order, tile_values.reshape(SLOTS, T, T), table, weight, bias_vec.reshape(1, 256), cotangent
    )
    return act, fgrad, wgrad, bgrad[:2].reshape(256)


def solution(mesh):
    return jax.shard_map(
        local,
        mesh=mesh,
        in_specs=(
            P(("rep", "row"), None),
            P(("rep", "row"), None),
            P("rep", "row", None, None, None),
            P("rep", "row", None),
            P("rep", "row", None),
            P("rep", "row"),
            P(),
            P(),
            P(("rep", "row"), None),
        ),
        out_specs=(P(("rep", "row"), None), P(("rep", "row"), None), P(), P()),
        check_vma=False,
    )
```

```python
import functools

import jax
import jax.numpy as jnp
from jax import lax
from jax.experimental import pallas as pl
from jax.experimental.pallas import tpu as pltpu
from jax.sharding import PartitionSpec as P

MESH = pl.DeviceIdType.MESH
NX, NY, NZ = 4, 8, 8
T = 128
R1, R2 = 32, 96
SLOTS = 135
GROUPS = ((0, 1), (1, 4), (5, 3))
GROUP_OF = (0, 1, 1, 1, 1, 2, 2, 2)
DIRECT = ()
ROWS = 64 * (R1 + R2)


def row1(ab, d, xi):
    return ((ab * 8 + d) * 4 + xi) * R1


def row2(ab, xi, d):
    return 64 * R1 + ((ab * 4 + xi) * 8 + d) * R2


PLAN = (
    (0, "z"), (0, "y2s"), (0, "o0"), (2, "ar1"), (0, "x1s"), (0, "pl0"), (0, "y2f"), (0, "o1"), (1, "x1s"),
    (1, "y2s"), (0, "y1n1"), (0, "y1n2"), (1, "o0"), (2, "ar2"), (0, "l0"), (0, "o2"), (0, "pl1"), (0, "pr1"),
    (1, "y2f"), (1, "o1"), (0, "pr0"), (1, "pr0"), (1, "y1n2"), (2, "ar3"), (0, "m0"), (0, "pr2"), (0, "pl2"),
    (1, "pl0"), (0, "y1f"), (0, "y1b"), (0, "l1"), (1, "y1n1"), (1, "o2"), (0, "m3"), (1, "pr1"), (1, "pl1"),
    (0, "m1"), (0, "m4"), (1, "y1f"), (1, "l0"), (0, "l2"), (0, "m2"), (0, "y1l"), (2, "ar4"), (1, "pr2"), (1, "y1b"),
    (1, "pl2"), (1, "m0"), (1, "l1"), (0, "m7"), (0, "m5"), (0, "m6"), (1, "m1"), (1, "y1l"), (1, "m2"), (1, "l2"),
    (2, "ar5"), (1, "m3"), (1, "m4"), (1, "m6"), (1, "m7"), (1, "m5"),
)


SEM_Z = 0


def sem_x1(ab):
    return 1 + ab


def sem_y1(ab, step):
    return 3 + ab * 3 + step


def sem_y2(ab, step):
    return 9 + ab * 2 + step


def sem_x2(ab, xi, g):
    return 13 + (ab * 3 + xi - 1) * 3 + g


def sem_sib(ab, g):
    return 31 + ab * 3 + g


N_RECV = 37
SEND_Z, SEND_X1, SEND_Y1, SEND_Y2, SEND_X2, SEND_SIB = range(6)


def kernel(
    features_hbm, order_hbm, tiles_hbm, table, weight_hbm, bias_hbm, cotangent_hbm,
    act_out, fgrad_out, wgrad_out, bgrad_out,
    features, order, weight, bias, cotangent,
    tiles, G, acc, part, part_in, wp, wp_in, w2, w2_in, w3, w3_in, wq, wfull,
    load_sem, recv, send, rs_recv, rs_send, ar_recv, ar_send,
):
    q = lax.axis_index("rep")
    r = lax.axis_index("row")
    y, zh, x, c = r // 16, (r // 8) % 2, (r // 2) % 4, r % 2
    z = zh * 4 + q

    def dev(dy=0, dx=0, dc=0):
        ny, nx, nc = (y + dy) % NY, (x + dx) % NX, (c + dc) % 2
        return (q, ny * 16 + zh * 8 + nx * 2 + nc)

    def dev_z(dz):
        nz = (z + dz) % NZ
        return (nz % 4, y * 16 + (nz // 4) * 8 + x * 2 + c)

    def dev_rep(dq):
        return ((q + dq) % 4, r)

    z_partner = dev_z(4)
    along_y = {j: dev(dy=j % NY) for j in (-2, -1, 1, 2)}
    along_x = {j: dev(dx=j % NX) for j in (-1, 1, 2)}
    sibling = dev(dc=1)
    line_y = [dev(dy=j) for j in range(1, NY)]
    line_xc = [(dx, dc, dev(dx=dx, dc=dc)) for dx in range(NX) for dc in range(2) if dx or dc]
    line_z = [dev_z(j) for j in range(1, NZ)]

    barrier = pltpu.get_barrier_semaphore()
    for peer in line_y + [p for _, _, p in line_xc] + line_z:
        pl.semaphore_signal(barrier, inc=1, device_id=peer, device_id_type=MESH)

    loads = [
        pltpu.make_async_copy(src, dst, load_sem.at[i]) for i, (src, dst) in enumerate((
            (features_hbm, features), (order_hbm, order), (tiles_hbm, tiles.at[pl.ds(0, SLOTS)]),
            (weight_hbm, weight), (bias_hbm, bias), (cotangent_hbm, cotangent),
        ))
    ]
    for load in loads:
        load.start()
    tiles[SLOTS] = jnp.zeros((T, T), jnp.bfloat16)

    acc[...] = jnp.zeros_like(acc)
    loads[0].wait()
    loads[1].wait()
    places = lax.broadcasted_iota(jnp.int32, (T, T), 0) == order[...]
    onehot = places.astype(jnp.float32).astype(jnp.bfloat16)

    def store_own(p, block):
        G[p, 0, pl.ds(row1(0, 0, 0), R1)] = block[:R1]
        G[p, 0, pl.ds(row2(0, 0, 0), R2)] = block[R1:]

    store_own(0, lax.dot_general(
        onehot, features[...], (((0,), (0,)), ((), ())), preferred_element_type=jnp.float32
    ).astype(jnp.bfloat16))

    pl.semaphore_wait(barrier, 21)

    def push(src, dst, send_sem, recv_sem, device):
        pltpu.make_async_remote_copy(
            src_ref=src, dst_ref=dst, send_sem=send_sem, recv_sem=recv_sem,
            device_id=device, device_id_type=MESH,
        ).start()

    def await_ref(ref, sem):
        pltpu.make_async_copy(ref, ref, sem).wait()

    def steps(p):
        own = G.at[p, 0]
        other = G.at[p, 1]
        waited = set()

        def go(src, dst, n, kind, sem, device):
            push(own.at[pl.ds(src, n)], own.at[pl.ds(dst, n)], send.at[p, kind], recv.at[p, sem], device)

        def ensure(sem, n):
            if sem not in waited:
                waited.add(sem)
                await_ref(own.at[pl.ds(0, n)], recv.at[p, sem])

        def sib(at, n, ab, g):
            push(own.at[pl.ds(at, n)], other.at[pl.ds(at, n)], send.at[p, SEND_SIB], recv.at[p, sem_sib(ab, g)], sibling)

        def sib1(ab, d, n, g):
            sib(row1(ab, d, 0), n * 4 * R1, ab, g)

        def sib2(ab, xi, g):
            sib(row2(ab, xi, GROUPS[g][0]), GROUPS[g][1] * R2, ab, g)

        def y1(ab, src, dst, step, dy):
            go(row1(ab, src, 0), row1(ab, dst, 0), 4 * R1, SEND_Y1, sem_y1(ab, step), along_y[dy])

        def y2(ab, src, dst, step, dy):
            go(row2(ab, 0, src), row2(ab, 0, dst), R2, SEND_Y2, sem_y2(ab, step), along_y[dy])

        def x2(ab, src, dst, g, dx, first=0, n=None):
            d, n = GROUPS[g][0] + first, GROUPS[g][1] if n is None else n
            if n:
                go(row2(ab, src, d), row2(ab, dst, d), n * R2, SEND_X2, sem_x2(ab, dst, g), along_x[dx])

        def own_ready(ab):
            if ab == 1:
                ensure(SEM_Z, R1 + R2)

        def partner():
            go(row1(0, 0, 0), row1(1, 0, 0), R1, SEND_Z, SEM_Z, z_partner)
            go(row2(0, 0, 0), row2(1, 0, 0), R2, SEND_Z, SEM_Z, z_partner)

        def y2_start(ab):
            own_ready(ab)
            for dst, dy in ((3, 2), (4, -2), (1, 1), (2, -1)):
                y2(ab, 0, dst, 0, dy)

        def x1_start(ab):
            own_ready(ab)
            for dx, xi in ((2, 3), (1, 1), (-1, 2)):
                go(row1(ab, 0, 0), row1(ab, 0, xi), R1, SEND_X1, sem_x1(ab), along_x[dx])

        def x2_own(ab, g):
            if g == 0:
                own_ready(ab)
            else:
                ensure(sem_y2(ab, g - 1), (4, 3)[g - 1] * R2)
            if (ab, g) in DIRECT:
                x2(ab, 0, 3, g, 2)
            x2(ab, 0, 1, g, 1)
            x2(ab, 0, 2, g, -1)
            sib2(ab, 0, g)

        def x2_pass(ab, g, xi):
            n = GROUPS[g][1]
            half = (n + 1 - ab) // 2
            ensure(sem_x2(ab, xi, g), n * R2)
            if (ab, g) not in DIRECT:
                if xi == 1:
                    x2(ab, 1, 3, g, 1, 0, half)
                else:
                    x2(ab, 2, 3, g, -1, half, n - half)
            sib2(ab, xi, g)

        def x2_last(ab, g):
            ensure(sem_x2(ab, 3, g), GROUPS[g][1] * R2)
            sib2(ab, 3, g)

        def y1_two(ab):
            ensure(sem_x1(ab), 3 * R1)
            y1(ab, 0, 3, 1, 2)
            y1(ab, 0, 4, 1, -2)

        def y1_one(ab):
            ensure(sem_x1(ab), 3 * R1)
            y1(ab, 0, 1, 0, 1)
            y1(ab, 0, 2, 0, -1)
            sib1(ab, 0, 1, 0)

        def y1_near(ab):
            ensure(sem_y1(ab, 0), 8 * R1)
            sib1(ab, 1, 2, 1)

        def y1_far(ab):
            ensure(sem_y1(ab, 1), 8 * R1)
            if ab == 0:
                y1(ab, 3, 7, 2, 2)
            else:
                y1(ab, 4, 7, 2, -2)
            y1(ab, 3, 5, 2, 1)
            y1(ab, 4, 6, 2, -1)
            sib1(ab, 3, 2, 1)

        def y1_last(ab):
            ensure(sem_y1(ab, 2), 12 * R1)
            sib1(ab, 5, 3, 2)

        def y2_far(ab):
            ensure(sem_y2(ab, 0), 4 * R2)
            if ab == 0:
                y2(ab, 3, 7, 1, 2)
            else:
                y2(ab, 4, 7, 1, -2)
            y2(ab, 3, 5, 1, 1)
            y2(ab, 4, 6, 1, -1)

        def mul(ab, d):
            g = GROUP_OF[d]
            ensure(sem_sib(ab, g), GROUPS[g][1] * 512)
            base = (ab * 8 + d) * 32
            left = jnp.concatenate([
                jnp.concatenate([tiles[table[base + col * 4 + j]] for col in range(8)], axis=1) for j in range(4)
            ], axis=0)
            pieces = []
            for xi in range(4):
                for k in range(2):
                    pieces.append(G[p, k, pl.ds(row1(ab, d, xi), R1)])
                    pieces.append(G[p, k, pl.ds(row2(ab, xi, d), R2)])
            acc[...] += jnp.dot(left, jnp.concatenate(pieces, axis=0), preferred_element_type=jnp.float32)

        def finish():
            for kind, n in ((SEND_Z, R1 + R2), (SEND_X1, 6 * R1), (SEND_Y1, 56 * R1), (SEND_Y2, 14 * R2), (SEND_X2, 48 * R2), (SEND_SIB, ROWS)):
                await_ref(own.at[pl.ds(0, n)], send.at[p, kind])

        named = {
            "y2s": y2_start, "x1s": x1_start, "y1n2": y1_two, "y1n1": y1_one, "y1b": y1_near, "y1f": y1_far,
            "y1l": y1_last, "y2f": y2_far, "z": lambda ab: partner(),
        }
        for g in range(3):
            named[f"o{g}"] = functools.partial(lambda g, ab: x2_own(ab, g), g)
            named[f"pl{g}"] = functools.partial(lambda g, ab: x2_pass(ab, g, 1), g)
            named[f"pr{g}"] = functools.partial(lambda g, ab: x2_pass(ab, g, 2), g)
            named[f"l{g}"] = functools.partial(lambda g, ab: x2_last(ab, g), g)
        for d in range(8):
            named[f"m{d}"] = functools.partial(lambda d, ab: mul(ab, d), d)
        return named, finish

    def run(p, sums, before_mul):
        named, finish = steps(p)
        for ab, word in PLAN:
            if word[0] == "m":
                before_mul()
            if ab < 2:
                named[word](ab)
            elif sums:
                sums[word]()
        return finish

    def reduce_rep(p):
        for j in range(1, 4):
            part[p, j - 1] = acc[pl.ds(j * T, T)].astype(jnp.bfloat16)
        for j in range(1, 4):
            push(part.at[p, j - 1], part_in.at[p, j - 1], rs_send.at[p], rs_recv.at[p], dev_rep(j))
        await_ref(part_in.at[p], rs_recv.at[p])
        total = acc[pl.ds(0, T)]
        for j in range(3):
            total = total + part_in[p, j].astype(jnp.float32)
        return total

    pending = list(loads[2:])

    def loaded():
        while pending:
            pending.pop().wait()

    finish0 = run(0, None, loaded)
    hidden = reduce_rep(0).astype(jnp.bfloat16)
    pre_act = jnp.dot(hidden, weight[...], preferred_element_type=jnp.float32) + bias[...]
    gate = jax.nn.sigmoid(pre_act)
    pre_grad = (cotangent[...].astype(jnp.float32) * gate * (1.0 + pre_act * (1.0 - gate))).astype(jnp.bfloat16)
    store_own(1, lax.dot_general(
        pre_grad, weight[...], (((1,), (1,)), ((), ())), preferred_element_type=jnp.float32
    ).astype(jnp.bfloat16))
    acc[...] = jnp.zeros_like(acc)

    def terms():
        act_out[...] = (pre_act * gate).astype(jnp.bfloat16)
        weight_term = lax.dot_general(
            hidden, pre_grad, (((0,), (0,)), ((), ())), preferred_element_type=jnp.float32
        )
        bias_term = jnp.sum(pre_grad.astype(jnp.float32), axis=0, keepdims=True)
        rows = lax.broadcasted_iota(jnp.int32, (8, T), 0)
        bias_tile = jnp.where(rows == 0, bias_term[:, :T], jnp.where(rows == 1, bias_term[:, T:], 0.0))
        for piece in range(NZ):
            for t in range(4):
                wp[piece, t] = weight_term[piece * 16 + (t // 2) * 8:piece * 16 + (t // 2) * 8 + 8, (t % 2) * T:(t % 2) * T + T]
            wp[piece, 4] = bias_tile

    def ar1():
        terms()
        for j in (4, 3, 5, 2, 6, 1, 7):
            push(wp.at[(z + j) % NZ], wp_in.at[j - 1], ar_send.at[0], ar_recv.at[0], dev_z(j))

    def ar2():
        await_ref(wp_in, ar_recv.at[0])
        total = wp[z]
        for j in range(NZ - 1):
            total = total + wp_in[j]
        for t in range(4):
            w2[t, 0] = total[t]
            w2[t, 1] = total[4]
        for dx, dc, device in line_xc:
            push(w2.at[(x + dx) % NX], w2_in.at[((NX - dx) % NX) * 2 + dc - 1], ar_send.at[1], ar_recv.at[1], device)

    def ar3():
        await_ref(w2_in, ar_recv.at[1])
        total = w2[x]
        for j in range(7):
            total = total + w2_in[j]
        w3[...] = total
        for j, device in enumerate(line_y):
            push(w3, w3_in.at[j], ar_send.at[2], ar_recv.at[2], device)

    def ar4():
        await_ref(w3_in, ar_recv.at[2])
        total = w3[...]
        for j in range(NY - 1):
            total = total + w3_in[j]
        bgrad_out[...] = total[1]
        wq[x] = total[0]
        for dx in range(1, NX):
            push(wq.at[x], wq.at[x], ar_send.at[3], ar_recv.at[3], dev(dx=dx))

    def ar5():
        await_ref(wq.at[pl.ds(0, NX - 1)], ar_recv.at[3])
        wfull[z] = wq[...]
        for j in (4, 3, 5, 2, 6, 1, 7):
            push(wfull.at[z], wfull.at[z], ar_send.at[4], ar_recv.at[4], dev_z(j))

    finish1 = run(1, {"ar1": ar1, "ar2": ar2, "ar3": ar3, "ar4": ar4, "ar5": ar5}, lambda: None)
    total = reduce_rep(1)
    grad = None
    for _ in range(3):
        piece = total.astype(jnp.bfloat16)
        total = total - piece.astype(jnp.float32)
        moved = jnp.dot(onehot, piece, preferred_element_type=jnp.float32)
        grad = moved if grad is None else grad + moved
    fgrad_out[...] = grad

    await_ref(wfull.at[pl.ds(0, NZ - 1)], ar_recv.at[4])
    for piece in range(8):
        for t in range(4):
            wgrad_out[pl.ds(piece * 16 + (t // 2) * 8, 8), pl.ds((t % 2) * T, T)] = wfull[piece, t]

    finish0()
    finish1()
    for p in range(2):
        await_ref(part.at[p], rs_send.at[p])
    await_ref(wp_in, ar_send.at[0])
    await_ref(w2_in, ar_send.at[1])
    await_ref(w3_in, ar_send.at[2])
    await_ref(wq.at[pl.ds(0, NX - 1)], ar_send.at[3])
    await_ref(wfull.at[pl.ds(0, NZ - 1)], ar_send.at[4])


def slot_table(tile_row, tile_col, tile_count):
    q = lax.axis_index("rep")
    r = lax.axis_index("row")
    y, zh, x, c = r // 16, (r // 8) % 2, (r // 2) % 4, r % 2
    place = jnp.arange(512, dtype=jnp.int32)
    j, k, xi, d, ab = place % 4, (place // 4) % 2, (place // 8) % 4, (place // 32) % 8, place // 256
    dy = jnp.where(d == 7, 4, jnp.where(d % 2 == 1, -((d + 1) // 2), d // 2))
    dx = jnp.where(xi == 3, 2, jnp.where(xi == 1, -1, xi // 2))
    col = ((y + dy) % NY) * 16 + (zh + ab) % 2 * 8 + ((x + dx) % NX) * 2 + (c + k) % 2
    want = col * 4 + (q + j) % 4
    have = tile_col.reshape(SLOTS) * 4 + tile_row.reshape(SLOTS)
    slots = jnp.arange(SLOTS, dtype=jnp.int32)
    hit = (want[:, None] == have[None, :]) & (slots[None, :] < tile_count.reshape(1, 1))
    return jnp.min(jnp.where(hit, slots[None, :], SLOTS), axis=1)


def local(
    features, node_order, tile_values, tile_row, tile_col, tile_count, weight, bias_vec, cotangent
):
    table = slot_table(tile_row, tile_col, tile_count)
    vmem = pl.BlockSpec(memory_space=pltpu.VMEM)
    hbm = pl.BlockSpec(memory_space=pl.ANY)
    act, fgrad, wgrad, bgrad = pl.pallas_call(
        kernel,
        out_shape=(
            jax.ShapeDtypeStruct((T, 256), jnp.bfloat16),
            jax.ShapeDtypeStruct((T, T), jnp.float32),
            jax.ShapeDtypeStruct((T, 256), jnp.float32),
            jax.ShapeDtypeStruct((8, T), jnp.float32),
        ),
        in_specs=[hbm, hbm, hbm, pl.BlockSpec(memory_space=pltpu.SMEM), hbm, hbm, hbm],
        out_specs=(vmem, vmem, vmem, vmem),
        scratch_shapes=[
            pltpu.VMEM((T, T), jnp.bfloat16),
            pltpu.VMEM((1, T), jnp.int32),
            pltpu.VMEM((T, 256), jnp.bfloat16),
            pltpu.VMEM((1, 256), jnp.float32),
            pltpu.VMEM((T, 256), jnp.bfloat16),
            pltpu.VMEM((SLOTS + 1, T, T), jnp.bfloat16),
            pltpu.VMEM((2, 2, ROWS, T), jnp.bfloat16),
            pltpu.VMEM((4 * T, T), jnp.float32),
            pltpu.VMEM((2, 3, T, T), jnp.bfloat16),
            pltpu.VMEM((2, 3, T, T), jnp.bfloat16),
            pltpu.VMEM((8, 5, 8, T), jnp.float32),
            pltpu.VMEM((NZ - 1, 5, 8, T), jnp.float32),
            pltpu.VMEM((NX, 2, 8, T), jnp.float32),
            pltpu.VMEM((7, 2, 8, T), jnp.float32),
            pltpu.VMEM((2, 8, T), jnp.float32),
            pltpu.VMEM((NY - 1, 2, 8, T), jnp.float32),
            pltpu.VMEM((NX, 8, T), jnp.float32),
            pltpu.VMEM((NZ, 4, 8, T), jnp.float32),
            pltpu.SemaphoreType.DMA((6,)),
            pltpu.SemaphoreType.DMA((2, N_RECV)),
            pltpu.SemaphoreType.DMA((2, 6)),
            pltpu.SemaphoreType.DMA((2,)),
            pltpu.SemaphoreType.DMA((2,)),
            pltpu.SemaphoreType.DMA((5,)),
            pltpu.SemaphoreType.DMA((5,)),
        ],
        compiler_params=pltpu.CompilerParams(
            collective_id=0, has_side_effects=True, vmem_limit_bytes=60 * 1024 * 1024
        ),
    )(
        features, node_order, tile_values.reshape(SLOTS, T, T), table, weight, bias_vec.reshape(1, 256), cotangent
    )
    return act, fgrad, wgrad, bgrad[:2].reshape(256)


def solution(mesh):
    return jax.shard_map(
        local,
        mesh=mesh,
        in_specs=(
            P(("rep", "row"), None),
            P(("rep", "row"), None),
            P("rep", "row", None, None, None),
            P("rep", "row", None),
            P("rep", "row", None),
            P("rep", "row"),
            P(),
            P(),
            P(("rep", "row"), None),
        ),
        out_specs=(P(("rep", "row"), None), P(("rep", "row"), None), P(), P()),
        check_vma=False,
    )
```

```python
import functools

import jax
import jax.numpy as jnp
from jax import lax
from jax.experimental import pallas as pl
from jax.experimental.pallas import tpu as pltpu
from jax.sharding import PartitionSpec as P

MESH = pl.DeviceIdType.MESH
NX, NY, NZ = 4, 8, 8
T = 128
R1, R2 = 32, 96
SLOTS = 135
GROUPS = ((0, 1), (1, 4), (5, 3))
GROUP_OF = (0, 1, 1, 1, 1, 2, 2, 2)
DIRECT = ()
ROWS = 64 * (R1 + R2)


def row1(ab, d, xi):
    return ((ab * 8 + d) * 4 + xi) * R1


def row2(ab, xi, d):
    return 64 * R1 + ((ab * 4 + xi) * 8 + d) * R2


PLAN = (
    (0, "z"), (0, "y2s"), (0, "o0"), (2, "ar1"), (0, "x1s"), (0, "pl0"), (0, "y2f"), (0, "o1"), (1, "x1s"),
    (1, "y2s"), (0, "y1n1"), (0, "y1n2"), (1, "o0"), (2, "ar2"), (0, "l0"), (0, "o2"), (0, "pl1"), (0, "pr1"),
    (1, "y2f"), (1, "o1"), (0, "pr0"), (1, "pr0"), (1, "y1n2"), (2, "ar3"), (0, "m0"), (0, "pr2"), (0, "pl2"),
    (1, "pl0"), (0, "y1f"), (0, "y1b"), (0, "l1"), (1, "y1n1"), (1, "o2"), (0, "m3"), (1, "pr1"), (1, "pl1"),
    (0, "m1"), (0, "m4"), (1, "y1f"), (1, "l0"), (0, "l2"), (0, "m2"), (0, "y1l"), (2, "ar4"), (1, "pr2"), (1, "y1b"),
    (1, "pl2"), (1, "m0"), (1, "l1"), (0, "m7"), (0, "m5"), (0, "m6"), (1, "m1"), (1, "y1l"), (1, "m2"), (1, "l2"),
    (2, "ar5"), (1, "m3"), (1, "m4"), (1, "m6"), (1, "m7"), (1, "m5"),
)


SEM_Z = 0


def sem_x1(ab):
    return 1 + ab


def sem_y1(ab, step):
    return 3 + ab * 3 + step


def sem_y2(ab, step):
    return 9 + ab * 2 + step


def sem_x2(ab, xi, g):
    return 13 + (ab * 3 + xi - 1) * 3 + g


def sem_sib(ab, g):
    return 31 + ab * 3 + g


N_RECV = 37
SEND_Z, SEND_X1, SEND_Y1, SEND_Y2, SEND_X2, SEND_SIB = range(6)


def kernel(
    features_hbm, order_hbm, tiles_hbm, row_hbm, col_hbm, count_hbm, weight_hbm, bias_hbm, cotangent_hbm,
    act_out, fgrad_out, wgrad_out, bgrad_out,
    features, order, weight, bias, cotangent, tile_row, tile_col, tile_count, found, table,
    tiles, G, acc, part, part_in, wp, wp_in, w2, w2_in, w3, w3_in, wq, wfull,
    load_sem, fill_sem, recv, send, rs_recv, rs_send, ar_recv, ar_send,
):
    q = lax.axis_index("rep")
    r = lax.axis_index("row")
    y, zh, x, c = r // 16, (r // 8) % 2, (r // 2) % 4, r % 2
    z = zh * 4 + q

    def dev(dy=0, dx=0, dc=0):
        ny, nx, nc = (y + dy) % NY, (x + dx) % NX, (c + dc) % 2
        return (q, ny * 16 + zh * 8 + nx * 2 + nc)

    def dev_z(dz):
        nz = (z + dz) % NZ
        return (nz % 4, y * 16 + (nz // 4) * 8 + x * 2 + c)

    def dev_rep(dq):
        return ((q + dq) % 4, r)

    z_partner = dev_z(4)
    along_y = {j: dev(dy=j % NY) for j in (-2, -1, 1, 2)}
    along_x = {j: dev(dx=j % NX) for j in (-1, 1, 2)}
    sibling = dev(dc=1)
    line_y = [dev(dy=j) for j in range(1, NY)]
    line_xc = [(dx, dc, dev(dx=dx, dc=dc)) for dx in range(NX) for dc in range(2) if dx or dc]
    line_z = [dev_z(j) for j in range(1, NZ)]

    barrier = pltpu.get_barrier_semaphore()
    for peer in line_y + [p for _, _, p in line_xc] + line_z:
        pl.semaphore_signal(barrier, inc=1, device_id=peer, device_id_type=MESH)

    loads = [
        pltpu.make_async_copy(src, dst, load_sem.at[i]) for i, (src, dst) in enumerate((
            (row_hbm, tile_row), (col_hbm, tile_col), (count_hbm, tile_count), (features_hbm, features), (order_hbm, order),
            (tiles_hbm, tiles.at[pl.ds(0, SLOTS)]), (weight_hbm, weight), (bias_hbm, bias), (cotangent_hbm, cotangent),
        ))
    ]
    for load in loads:
        load.start()
    tiles[SLOTS] = jnp.zeros((T, T), jnp.bfloat16)

    acc[...] = jnp.zeros_like(acc)
    for load in loads[:5]:
        load.wait()
    places = lax.broadcasted_iota(jnp.int32, (T, T), 0) == order[...]
    onehot = places.astype(jnp.float32).astype(jnp.bfloat16)

    def store_own(p, block):
        G[p, 0, pl.ds(row1(0, 0, 0), R1)] = block[:R1]
        G[p, 0, pl.ds(row2(0, 0, 0), R2)] = block[R1:]

    store_own(0, lax.dot_general(
        onehot, features[...], (((0,), (0,)), ((), ())), preferred_element_type=jnp.float32
    ).astype(jnp.bfloat16))

    place = lax.broadcasted_iota(jnp.int32, (4, T), 0) * T + lax.broadcasted_iota(jnp.int32, (4, T), 1)
    j, k, xi, d, ab = place & 3, (place >> 2) & 1, (place >> 3) & 3, (place >> 5) & 7, place >> 8
    dy = jnp.where(d == 7, 4, jnp.where((d & 1) == 1, -((d + 1) >> 1), d >> 1))
    dx = jnp.where(xi == 3, 2, jnp.where(xi == 1, -1, xi >> 1))
    column = ((y + dy) & 7) * 16 + ((zh + ab) & 1) * 8 + ((x + dx) & 3) * 2 + ((c + k) & 1)
    want = column * 4 + ((q + j) & 3)
    used = tile_count[0, 0]

    def look(slot, at):
        key = jnp.where(slot < used, tile_col[0, slot] * 4 + tile_row[0, slot], -1)
        return jnp.where(want == key, slot, at)

    found[...] = lax.fori_loop(0, SLOTS, look, jnp.full((4, T), SLOTS, jnp.int32), unroll=5)
    fill = pltpu.make_async_copy(found, table, fill_sem)
    fill.start()

    pl.semaphore_wait(barrier, 21)

    def push(src, dst, send_sem, recv_sem, device):
        pltpu.make_async_remote_copy(
            src_ref=src, dst_ref=dst, send_sem=send_sem, recv_sem=recv_sem,
            device_id=device, device_id_type=MESH,
        ).start()

    def await_ref(ref, sem):
        pltpu.make_async_copy(ref, ref, sem).wait()

    def steps(p):
        own = G.at[p, 0]
        other = G.at[p, 1]
        waited = set()

        def go(src, dst, n, kind, sem, device):
            push(own.at[pl.ds(src, n)], own.at[pl.ds(dst, n)], send.at[p, kind], recv.at[p, sem], device)

        def ensure(sem, n):
            if sem not in waited:
                waited.add(sem)
                await_ref(own.at[pl.ds(0, n)], recv.at[p, sem])

        def sib(at, n, ab, g):
            push(own.at[pl.ds(at, n)], other.at[pl.ds(at, n)], send.at[p, SEND_SIB], recv.at[p, sem_sib(ab, g)], sibling)

        def sib1(ab, d, n, g):
            sib(row1(ab, d, 0), n * 4 * R1, ab, g)

        def sib2(ab, xi, g):
            sib(row2(ab, xi, GROUPS[g][0]), GROUPS[g][1] * R2, ab, g)

        def y1(ab, src, dst, step, dy):
            go(row1(ab, src, 0), row1(ab, dst, 0), 4 * R1, SEND_Y1, sem_y1(ab, step), along_y[dy])

        def y2(ab, src, dst, step, dy):
            go(row2(ab, 0, src), row2(ab, 0, dst), R2, SEND_Y2, sem_y2(ab, step), along_y[dy])

        def x2(ab, src, dst, g, dx, first=0, n=None):
            d, n = GROUPS[g][0] + first, GROUPS[g][1] if n is None else n
            if n:
                go(row2(ab, src, d), row2(ab, dst, d), n * R2, SEND_X2, sem_x2(ab, dst, g), along_x[dx])

        def own_ready(ab):
            if ab == 1:
                ensure(SEM_Z, R1 + R2)

        def partner():
            go(row1(0, 0, 0), row1(1, 0, 0), R1, SEND_Z, SEM_Z, z_partner)
            go(row2(0, 0, 0), row2(1, 0, 0), R2, SEND_Z, SEM_Z, z_partner)

        def y2_start(ab):
            own_ready(ab)
            for dst, dy in ((3, 2), (4, -2), (1, 1), (2, -1)):
                y2(ab, 0, dst, 0, dy)

        def x1_start(ab):
            own_ready(ab)
            for dx, xi in ((2, 3), (1, 1), (-1, 2)):
                go(row1(ab, 0, 0), row1(ab, 0, xi), R1, SEND_X1, sem_x1(ab), along_x[dx])

        def x2_own(ab, g):
            if g == 0:
                own_ready(ab)
            else:
                ensure(sem_y2(ab, g - 1), (4, 3)[g - 1] * R2)
            if (ab, g) in DIRECT:
                x2(ab, 0, 3, g, 2)
            x2(ab, 0, 1, g, 1)
            x2(ab, 0, 2, g, -1)
            sib2(ab, 0, g)

        def x2_pass(ab, g, xi):
            n = GROUPS[g][1]
            half = (n + 1 - ab) // 2
            ensure(sem_x2(ab, xi, g), n * R2)
            if (ab, g) not in DIRECT:
                if xi == 1:
                    x2(ab, 1, 3, g, 1, 0, half)
                else:
                    x2(ab, 2, 3, g, -1, half, n - half)
            sib2(ab, xi, g)

        def x2_last(ab, g):
            ensure(sem_x2(ab, 3, g), GROUPS[g][1] * R2)
            sib2(ab, 3, g)

        def y1_two(ab):
            ensure(sem_x1(ab), 3 * R1)
            y1(ab, 0, 3, 1, 2)
            y1(ab, 0, 4, 1, -2)

        def y1_one(ab):
            ensure(sem_x1(ab), 3 * R1)
            y1(ab, 0, 1, 0, 1)
            y1(ab, 0, 2, 0, -1)
            sib1(ab, 0, 1, 0)

        def y1_near(ab):
            ensure(sem_y1(ab, 0), 8 * R1)
            sib1(ab, 1, 2, 1)

        def y1_far(ab):
            ensure(sem_y1(ab, 1), 8 * R1)
            if ab == 0:
                y1(ab, 3, 7, 2, 2)
            else:
                y1(ab, 4, 7, 2, -2)
            y1(ab, 3, 5, 2, 1)
            y1(ab, 4, 6, 2, -1)
            sib1(ab, 3, 2, 1)

        def y1_last(ab):
            ensure(sem_y1(ab, 2), 12 * R1)
            sib1(ab, 5, 3, 2)

        def y2_far(ab):
            ensure(sem_y2(ab, 0), 4 * R2)
            if ab == 0:
                y2(ab, 3, 7, 1, 2)
            else:
                y2(ab, 4, 7, 1, -2)
            y2(ab, 3, 5, 1, 1)
            y2(ab, 4, 6, 1, -1)

        def mul(ab, d):
            g = GROUP_OF[d]
            ensure(sem_sib(ab, g), GROUPS[g][1] * 512)
            base = (ab * 8 + d) * 32
            left = jnp.concatenate([
                jnp.concatenate([tiles[table[(base + col * 4 + j) // T, (base + col * 4 + j) % T]] for col in range(8)], axis=1) for j in range(4)
            ], axis=0)
            pieces = []
            for xi in range(4):
                for k in range(2):
                    pieces.append(G[p, k, pl.ds(row1(ab, d, xi), R1)])
                    pieces.append(G[p, k, pl.ds(row2(ab, xi, d), R2)])
            acc[...] += jnp.dot(left, jnp.concatenate(pieces, axis=0), preferred_element_type=jnp.float32)

        def finish():
            for kind, n in ((SEND_Z, R1 + R2), (SEND_X1, 6 * R1), (SEND_Y1, 56 * R1), (SEND_Y2, 14 * R2), (SEND_X2, 48 * R2), (SEND_SIB, ROWS)):
                await_ref(own.at[pl.ds(0, n)], send.at[p, kind])

        named = {
            "y2s": y2_start, "x1s": x1_start, "y1n2": y1_two, "y1n1": y1_one, "y1b": y1_near, "y1f": y1_far,
            "y1l": y1_last, "y2f": y2_far, "z": lambda ab: partner(),
        }
        for g in range(3):
            named[f"o{g}"] = functools.partial(lambda g, ab: x2_own(ab, g), g)
            named[f"pl{g}"] = functools.partial(lambda g, ab: x2_pass(ab, g, 1), g)
            named[f"pr{g}"] = functools.partial(lambda g, ab: x2_pass(ab, g, 2), g)
            named[f"l{g}"] = functools.partial(lambda g, ab: x2_last(ab, g), g)
        for d in range(8):
            named[f"m{d}"] = functools.partial(lambda d, ab: mul(ab, d), d)
        return named, finish

    def run(p, sums, before_mul):
        named, finish = steps(p)
        for ab, word in PLAN:
            if word[0] == "m":
                before_mul()
            if ab < 2:
                named[word](ab)
            elif sums:
                sums[word]()
        return finish

    def reduce_rep(p):
        for j in range(1, 4):
            part[p, j - 1] = acc[pl.ds(j * T, T)].astype(jnp.bfloat16)
        for j in (3, 2, 1):
            push(part.at[p, j - 1], part_in.at[p, j - 1], rs_send.at[p], rs_recv.at[p], dev_rep(j))
        await_ref(part_in.at[p], rs_recv.at[p])
        total = acc[pl.ds(0, T)]
        for j in range(3):
            total = total + part_in[p, j].astype(jnp.float32)
        return total

    pending = [fill] + loads[5:]

    def loaded():
        while pending:
            pending.pop().wait()

    finish0 = run(0, None, loaded)
    hidden = reduce_rep(0).astype(jnp.bfloat16)
    pre_act = jnp.dot(hidden, weight[...], preferred_element_type=jnp.float32) + bias[...]
    gate = jax.nn.sigmoid(pre_act)
    pre_grad = (cotangent[...].astype(jnp.float32) * gate * (1.0 + pre_act * (1.0 - gate))).astype(jnp.bfloat16)
    store_own(1, lax.dot_general(
        pre_grad, weight[...], (((1,), (1,)), ((), ())), preferred_element_type=jnp.float32
    ).astype(jnp.bfloat16))
    acc[...] = jnp.zeros_like(acc)

    def terms():
        act_out[...] = (pre_act * gate).astype(jnp.bfloat16)
        weight_term = lax.dot_general(
            hidden, pre_grad, (((0,), (0,)), ((), ())), preferred_element_type=jnp.float32
        )
        bias_term = jnp.sum(pre_grad.astype(jnp.float32), axis=0, keepdims=True)
        rows = lax.broadcasted_iota(jnp.int32, (8, T), 0)
        bias_tile = jnp.where(rows == 0, bias_term[:, :T], jnp.where(rows == 1, bias_term[:, T:], 0.0))
        for piece in range(NZ):
            for t in range(4):
                wp[piece, t] = weight_term[piece * 16 + (t // 2) * 8:piece * 16 + (t // 2) * 8 + 8, (t % 2) * T:(t % 2) * T + T]
            wp[piece, 4] = bias_tile

    def ar1():
        terms()
        for j in (4, 3, 5, 2, 6, 1, 7):
            push(wp.at[(z + j) % NZ], wp_in.at[j - 1], ar_send.at[0], ar_recv.at[0], dev_z(j))

    def ar2():
        await_ref(wp_in, ar_recv.at[0])
        total = wp[z]
        for j in range(NZ - 1):
            total = total + wp_in[j]
        for t in range(4):
            w2[t, 0] = total[t]
            w2[t, 1] = total[4]
        for dx, dc, device in line_xc:
            push(w2.at[(x + dx) % NX], w2_in.at[((NX - dx) % NX) * 2 + dc - 1], ar_send.at[1], ar_recv.at[1], device)

    def ar3():
        await_ref(w2_in, ar_recv.at[1])
        total = w2[x]
        for j in range(7):
            total = total + w2_in[j]
        w3[...] = total
        for j, device in enumerate(line_y):
            push(w3, w3_in.at[j], ar_send.at[2], ar_recv.at[2], device)

    def ar4():
        await_ref(w3_in, ar_recv.at[2])
        total = w3[...]
        for j in range(NY - 1):
            total = total + w3_in[j]
        bgrad_out[:, :T] = total[1, 0:1]
        bgrad_out[:, T:] = total[1, 1:2]
        wq[x] = total[0]
        for dx in range(1, NX):
            push(wq.at[x], wq.at[x], ar_send.at[3], ar_recv.at[3], dev(dx=dx))

    def ar5():
        await_ref(wq.at[pl.ds(0, NX - 1)], ar_recv.at[3])
        wfull[z] = wq[...]
        for j in (4, 3, 5, 2, 6, 1, 7):
            push(wfull.at[z], wfull.at[z], ar_send.at[4], ar_recv.at[4], dev_z(j))

    finish1 = run(1, {"ar1": ar1, "ar2": ar2, "ar3": ar3, "ar4": ar4, "ar5": ar5}, lambda: None)
    total = reduce_rep(1)
    grad = None
    for _ in range(3):
        piece = total.astype(jnp.bfloat16)
        total = total - piece.astype(jnp.float32)
        moved = jnp.dot(onehot, piece, preferred_element_type=jnp.float32)
        grad = moved if grad is None else grad + moved
    fgrad_out[...] = grad

    await_ref(wfull.at[pl.ds(0, NZ - 1)], ar_recv.at[4])
    for piece in range(8):
        for t in range(4):
            wgrad_out[pl.ds(piece * 16 + (t // 2) * 8, 8), pl.ds((t % 2) * T, T)] = wfull[piece, t]

    finish0()
    finish1()
    for p in range(2):
        await_ref(part.at[p], rs_send.at[p])
    await_ref(wp_in, ar_send.at[0])
    await_ref(w2_in, ar_send.at[1])
    await_ref(w3_in, ar_send.at[2])
    await_ref(wq.at[pl.ds(0, NX - 1)], ar_send.at[3])
    await_ref(wfull.at[pl.ds(0, NZ - 1)], ar_send.at[4])


def publish(*refs):
    sources, targets, staged, sems = refs[:4], refs[4:8], refs[8:12], refs[12]
    reads = [pltpu.make_async_copy(sources[i], staged[i], sems.at[0, i]) for i in range(4)]
    writes = [pltpu.make_async_copy(staged[i], targets[i], sems.at[1, i]) for i in range(4)]
    for copy in reads:
        copy.start()
    for read, write in zip(reads, writes):
        read.wait()
        write.start()
    for copy in writes:
        copy.wait()


def local(
    features, node_order, tile_values, tile_row, tile_col, tile_count, weight, bias_vec, cotangent
):
    vmem = pl.BlockSpec(memory_space=pltpu.VMEM)
    hbm = pl.BlockSpec(memory_space=pl.ANY)
    act, fgrad, wgrad, bgrad = pl.pallas_call(
        kernel,
        out_shape=(
            jax.ShapeDtypeStruct((T, 256), jnp.bfloat16),
            jax.ShapeDtypeStruct((T, T), jnp.float32),
            jax.ShapeDtypeStruct((T, 256), jnp.float32),
            jax.ShapeDtypeStruct((1, 256), jnp.float32),
        ),
        in_specs=[hbm] * 9,
        out_specs=(vmem, vmem, vmem, vmem),
        scratch_shapes=[
            pltpu.VMEM((T, T), jnp.bfloat16),
            pltpu.VMEM((1, T), jnp.int32),
            pltpu.VMEM((T, 256), jnp.bfloat16),
            pltpu.VMEM((1, 256), jnp.float32),
            pltpu.VMEM((T, 256), jnp.bfloat16),
            pltpu.SMEM((1, SLOTS), jnp.int32),
            pltpu.SMEM((1, SLOTS), jnp.int32),
            pltpu.SMEM((1, 1), jnp.int32),
            pltpu.VMEM((4, T), jnp.int32),
            pltpu.SMEM((4, T), jnp.int32),
            pltpu.VMEM((SLOTS + 1, T, T), jnp.bfloat16),
            pltpu.VMEM((2, 2, ROWS, T), jnp.bfloat16),
            pltpu.VMEM((4 * T, T), jnp.float32),
            pltpu.VMEM((2, 3, T, T), jnp.bfloat16),
            pltpu.VMEM((2, 3, T, T), jnp.bfloat16),
            pltpu.VMEM((8, 5, 8, T), jnp.float32),
            pltpu.VMEM((NZ - 1, 5, 8, T), jnp.float32),
            pltpu.VMEM((NX, 2, 8, T), jnp.float32),
            pltpu.VMEM((7, 2, 8, T), jnp.float32),
            pltpu.VMEM((2, 8, T), jnp.float32),
            pltpu.VMEM((NY - 1, 2, 8, T), jnp.float32),
            pltpu.VMEM((NX, 8, T), jnp.float32),
            pltpu.VMEM((NZ, 4, 8, T), jnp.float32),
            pltpu.SemaphoreType.DMA((9,)),
            pltpu.SemaphoreType.DMA,
            pltpu.SemaphoreType.DMA((2, N_RECV)),
            pltpu.SemaphoreType.DMA((2, 6)),
            pltpu.SemaphoreType.DMA((2,)),
            pltpu.SemaphoreType.DMA((2,)),
            pltpu.SemaphoreType.DMA((5,)),
            pltpu.SemaphoreType.DMA((5,)),
        ],
        compiler_params=pltpu.CompilerParams(
            collective_id=0, has_side_effects=True, vmem_limit_bytes=60 * 1024 * 1024
        ),
    )(
        features, node_order, tile_values.reshape(SLOTS, T, T), tile_row.reshape(1, SLOTS), tile_col.reshape(1, SLOTS),
        tile_count, weight, bias_vec.reshape(1, 256), cotangent,
    )
    anywhere = pl.BlockSpec(memory_space=pl.ANY)
    act, fgrad, wgrad, bgrad = pl.pallas_call(
        publish,
        out_shape=tuple(jax.ShapeDtypeStruct(a.shape, a.dtype) for a in (act, fgrad, wgrad, bgrad)),
        in_specs=[anywhere] * 4,
        out_specs=(anywhere,) * 4,
        scratch_shapes=[pltpu.VMEM(a.shape, a.dtype) for a in (act, fgrad, wgrad, bgrad)] + [pltpu.SemaphoreType.DMA((2, 4))],
        compiler_params=pltpu.CompilerParams(vmem_limit_bytes=60 * 1024 * 1024),
    )(act, fgrad, wgrad, bgrad)
    return act, fgrad, wgrad, bgrad.reshape(256)


def solution(mesh):
    return jax.shard_map(
        local,
        mesh=mesh,
        in_specs=(
            P(("rep", "row"), None),
            P(("rep", "row"), None),
            P("rep", "row", None, None, None),
            P("rep", "row", None),
            P("rep", "row", None),
            P("rep", "row"),
            P(),
            P(),
            P(("rep", "row"), None),
        ),
        out_specs=(P(("rep", "row"), None), P(("rep", "row"), None), P(), P()),
        check_vma=False,
    )
```

```python
import functools

import jax
import jax.numpy as jnp
from jax import lax
from jax.experimental import pallas as pl
from jax.experimental.pallas import tpu as pltpu
from jax.sharding import PartitionSpec as P

MESH = pl.DeviceIdType.MESH
NX, NY, NZ = 4, 8, 8
T = 128
R1, R2 = 32, 96
SLOTS = 135
GROUPS = ((0, 1), (1, 4), (5, 3))
GROUP_OF = (0, 1, 1, 1, 1, 2, 2, 2)
DIRECT = ()
ROWS = 64 * (R1 + R2)


def row1(ab, d, xi):
    return ((ab * 8 + d) * 4 + xi) * R1


def row2(ab, xi, d):
    return 64 * R1 + ((ab * 4 + xi) * 8 + d) * R2


PLAN = (
    (0, "z"), (0, "y2s"), (0, "o0"), (2, "ar1"), (0, "x1s"), (0, "pl0"), (0, "y2f"), (0, "o1"), (1, "x1s"),
    (1, "y2s"), (0, "y1n1"), (0, "y1n2"), (1, "o0"), (2, "ar2"), (0, "l0"), (0, "o2"), (0, "pl1"), (0, "pr1"),
    (1, "y2f"), (1, "o1"), (0, "pr0"), (1, "pr0"), (1, "y1n2"), (2, "ar3"), (0, "m0"), (0, "pr2"), (0, "pl2"),
    (1, "pl0"), (0, "y1f"), (0, "y1b"), (0, "l1"), (1, "y1n1"), (1, "o2"), (0, "m3"), (1, "pr1"), (1, "pl1"),
    (0, "m1"), (0, "m4"), (1, "y1f"), (1, "l0"), (0, "l2"), (0, "m2"), (0, "y1l"), (2, "ar4"), (1, "pr2"), (1, "y1b"),
    (1, "pl2"), (1, "m0"), (1, "l1"), (0, "m7"), (0, "m5"), (0, "m6"), (1, "m1"), (1, "y1l"), (1, "m2"), (1, "l2"),
    (2, "ar5"), (1, "m3"), (1, "m4"), (1, "m6"), (1, "m7"), (1, "m5"),
)


SEM_Z = 0


def sem_x1(ab):
    return 1 + ab


def sem_y1(ab, step):
    return 3 + ab * 3 + step


def sem_y2(ab, step):
    return 9 + ab * 2 + step


def sem_x2(ab, xi, g):
    return 13 + (ab * 3 + xi - 1) * 3 + g


def sem_sib(ab, g):
    return 31 + ab * 3 + g


N_RECV = 37
SEND_Z, SEND_X1, SEND_Y1, SEND_Y2, SEND_X2, SEND_SIB = range(6)


def kernel(
    features_hbm, order_hbm, tiles_hbm, row_hbm, col_hbm, count_hbm, weight_hbm, bias_hbm, cotangent_hbm,
    act_out, fgrad_out, wgrad_out, bgrad_out,
    features, order, weight, bias, cotangent, tile_row, tile_col, tile_count, found, table,
    tiles, G, acc, part, part_in, wp, wp_in, w2, w2_in, w3, w3_in, wq, wfull,
    load_sem, fill_sem, recv, send, rs_recv, rs_send, ar_recv, ar_send,
):
    q = lax.axis_index("rep")
    r = lax.axis_index("row")
    y, zh, x, c = r // 16, (r // 8) % 2, (r // 2) % 4, r % 2
    z = zh * 4 + q

    def dev(dy=0, dx=0, dc=0):
        ny, nx, nc = (y + dy) % NY, (x + dx) % NX, (c + dc) % 2
        return (q, ny * 16 + zh * 8 + nx * 2 + nc)

    def dev_z(dz):
        nz = (z + dz) % NZ
        return (nz % 4, y * 16 + (nz // 4) * 8 + x * 2 + c)

    def dev_rep(dq):
        return ((q + dq) % 4, r)

    z_partner = dev_z(4)
    along_y = {j: dev(dy=j % NY) for j in (-2, -1, 1, 2)}
    along_x = {j: dev(dx=j % NX) for j in (-1, 1, 2)}
    sibling = dev(dc=1)
    line_y = [dev(dy=j) for j in range(1, NY)]
    line_xc = [(dx, dc, dev(dx=dx, dc=dc)) for dx in range(NX) for dc in range(2) if dx or dc]
    line_z = [dev_z(j) for j in range(1, NZ)]

    barrier = pltpu.get_barrier_semaphore()
    for peer in line_y + [p for _, _, p in line_xc] + line_z:
        pl.semaphore_signal(barrier, inc=1, device_id=peer, device_id_type=MESH)

    loads = [
        pltpu.make_async_copy(src, dst, load_sem.at[i]) for i, (src, dst) in enumerate((
            (row_hbm, tile_row), (col_hbm, tile_col), (count_hbm, tile_count), (features_hbm, features), (order_hbm, order),
            (tiles_hbm, tiles.at[pl.ds(0, SLOTS)]), (weight_hbm, weight), (bias_hbm, bias), (cotangent_hbm, cotangent),
        ))
    ]
    for load in loads:
        load.start()
    tiles[SLOTS] = jnp.zeros((T, T), jnp.bfloat16)

    acc[...] = jnp.zeros_like(acc)
    for load in loads[:5]:
        load.wait()
    places = lax.broadcasted_iota(jnp.int32, (T, T), 0) == order[...]
    onehot = places.astype(jnp.float32).astype(jnp.bfloat16)

    def store_own(p, block):
        G[p, 0, pl.ds(row1(0, 0, 0), R1)] = block[:R1]
        G[p, 0, pl.ds(row2(0, 0, 0), R2)] = block[R1:]

    store_own(0, lax.dot_general(
        onehot, features[...], (((0,), (0,)), ((), ())), preferred_element_type=jnp.float32
    ).astype(jnp.bfloat16))

    place = lax.broadcasted_iota(jnp.int32, (4, T), 0) * T + lax.broadcasted_iota(jnp.int32, (4, T), 1)
    j, k, xi, d, ab = place & 3, (place >> 2) & 1, (place >> 3) & 3, (place >> 5) & 7, place >> 8
    dy = jnp.where(d == 7, 4, jnp.where((d & 1) == 1, -((d + 1) >> 1), d >> 1))
    dx = jnp.where(xi == 3, 2, jnp.where(xi == 1, -1, xi >> 1))
    column = ((y + dy) & 7) * 16 + ((zh + ab) & 1) * 8 + ((x + dx) & 3) * 2 + ((c + k) & 1)
    want = column * 4 + ((q + j) & 3)
    used = tile_count[0, 0]

    def look(slot, at):
        key = jnp.where(slot < used, tile_col[0, slot] * 4 + tile_row[0, slot], -1)
        return jnp.where(want == key, slot, at)

    found[...] = lax.fori_loop(0, SLOTS, look, jnp.full((4, T), SLOTS, jnp.int32), unroll=5)
    fill = pltpu.make_async_copy(found, table, fill_sem)
    fill.start()

    pl.semaphore_wait(barrier, 21)

    def push(src, dst, send_sem, recv_sem, device):
        pltpu.make_async_remote_copy(
            src_ref=src, dst_ref=dst, send_sem=send_sem, recv_sem=recv_sem,
            device_id=device, device_id_type=MESH,
        ).start()

    def await_ref(ref, sem):
        pltpu.make_async_copy(ref, ref, sem).wait()

    def steps(p):
        own = G.at[p, 0]
        other = G.at[p, 1]
        waited = set()

        def go(src, dst, n, kind, sem, device):
            push(own.at[pl.ds(src, n)], own.at[pl.ds(dst, n)], send.at[p, kind], recv.at[p, sem], device)

        def ensure(sem, n):
            if sem not in waited:
                waited.add(sem)
                await_ref(own.at[pl.ds(0, n)], recv.at[p, sem])

        def sib(at, n, ab, g):
            push(own.at[pl.ds(at, n)], other.at[pl.ds(at, n)], send.at[p, SEND_SIB], recv.at[p, sem_sib(ab, g)], sibling)

        def sib1(ab, d, n, g):
            sib(row1(ab, d, 0), n * 4 * R1, ab, g)

        def sib2(ab, xi, g):
            sib(row2(ab, xi, GROUPS[g][0]), GROUPS[g][1] * R2, ab, g)

        def y1(ab, src, dst, step, dy):
            go(row1(ab, src, 0), row1(ab, dst, 0), 4 * R1, SEND_Y1, sem_y1(ab, step), along_y[dy])

        def y2(ab, src, dst, step, dy):
            go(row2(ab, 0, src), row2(ab, 0, dst), R2, SEND_Y2, sem_y2(ab, step), along_y[dy])

        def x2(ab, src, dst, g, dx, first=0, n=None):
            d, n = GROUPS[g][0] + first, GROUPS[g][1] if n is None else n
            if n:
                go(row2(ab, src, d), row2(ab, dst, d), n * R2, SEND_X2, sem_x2(ab, dst, g), along_x[dx])

        def own_ready(ab):
            if ab == 1:
                ensure(SEM_Z, R1 + R2)

        def partner():
            go(row1(0, 0, 0), row1(1, 0, 0), R1, SEND_Z, SEM_Z, z_partner)
            go(row2(0, 0, 0), row2(1, 0, 0), R2, SEND_Z, SEM_Z, z_partner)

        def y2_start(ab):
            own_ready(ab)
            for dst, dy in ((3, 2), (4, -2), (1, 1), (2, -1)):
                y2(ab, 0, dst, 0, dy)

        def x1_start(ab):
            own_ready(ab)
            for dx, xi in ((2, 3), (1, 1), (-1, 2)):
                go(row1(ab, 0, 0), row1(ab, 0, xi), R1, SEND_X1, sem_x1(ab), along_x[dx])

        def x2_own(ab, g):
            if g == 0:
                own_ready(ab)
            else:
                ensure(sem_y2(ab, g - 1), (4, 3)[g - 1] * R2)
            if (ab, g) in DIRECT:
                x2(ab, 0, 3, g, 2)
            x2(ab, 0, 1, g, 1)
            x2(ab, 0, 2, g, -1)
            sib2(ab, 0, g)

        def x2_pass(ab, g, xi):
            n = GROUPS[g][1]
            half = (n + 1 - ab) // 2
            ensure(sem_x2(ab, xi, g), n * R2)
            if (ab, g) not in DIRECT:
                if xi == 1:
                    x2(ab, 1, 3, g, 1, 0, half)
                else:
                    x2(ab, 2, 3, g, -1, half, n - half)
            sib2(ab, xi, g)

        def x2_last(ab, g):
            ensure(sem_x2(ab, 3, g), GROUPS[g][1] * R2)
            sib2(ab, 3, g)

        def y1_two(ab):
            ensure(sem_x1(ab), 3 * R1)
            y1(ab, 0, 3, 1, 2)
            y1(ab, 0, 4, 1, -2)

        def y1_one(ab):
            ensure(sem_x1(ab), 3 * R1)
            y1(ab, 0, 1, 0, 1)
            y1(ab, 0, 2, 0, -1)
            sib1(ab, 0, 1, 0)

        def y1_near(ab):
            ensure(sem_y1(ab, 0), 8 * R1)
            sib1(ab, 1, 2, 1)

        def y1_far(ab):
            ensure(sem_y1(ab, 1), 8 * R1)
            if ab == 0:
                y1(ab, 3, 7, 2, 2)
            else:
                y1(ab, 4, 7, 2, -2)
            y1(ab, 3, 5, 2, 1)
            y1(ab, 4, 6, 2, -1)
            sib1(ab, 3, 2, 1)

        def y1_last(ab):
            ensure(sem_y1(ab, 2), 12 * R1)
            sib1(ab, 5, 3, 2)

        def y2_far(ab):
            ensure(sem_y2(ab, 0), 4 * R2)
            if ab == 0:
                y2(ab, 3, 7, 1, 2)
            else:
                y2(ab, 4, 7, 1, -2)
            y2(ab, 3, 5, 1, 1)
            y2(ab, 4, 6, 1, -1)

        def columns(ab, d):
            pieces = []
            for xi in range(4):
                for k in range(2):
                    pieces.append(G[p, k, pl.ds(row1(ab, d, xi), R1)])
                    pieces.append(G[p, k, pl.ds(row2(ab, xi, d), R2)])
            return pieces

        def blocks(ab, d, j):
            base = (ab * 8 + d) * 32 + j
            return [tiles[table[(base + col * 4) // T, (base + col * 4) % T]] for col in range(8)]

        def arrived(ab, d):
            g = GROUP_OF[d]
            ensure(sem_sib(ab, g), GROUPS[g][1] * 512)

        def mul(ab, d):
            arrived(ab, d)
            left = jnp.concatenate([jnp.concatenate(blocks(ab, d, j), axis=1) for j in range(4)], axis=0)
            acc[...] += jnp.dot(left, jnp.concatenate(columns(ab, d), axis=0), preferred_element_type=jnp.float32)

        def last_rows(places, j):
            total = acc[pl.ds(j * T, T)]
            for ab, d in places:
                arrived(ab, d)
                total = total + jnp.dot(
                    jnp.concatenate(blocks(ab, d, j), axis=1), jnp.concatenate(columns(ab, d), axis=0),
                    preferred_element_type=jnp.float32,
                )
            return total

        def finish():
            for kind, n in ((SEND_Z, R1 + R2), (SEND_X1, 6 * R1), (SEND_Y1, 56 * R1), (SEND_Y2, 14 * R2), (SEND_X2, 48 * R2), (SEND_SIB, ROWS)):
                await_ref(own.at[pl.ds(0, n)], send.at[p, kind])

        named = {
            "y2s": y2_start, "x1s": x1_start, "y1n2": y1_two, "y1n1": y1_one, "y1b": y1_near, "y1f": y1_far,
            "y1l": y1_last, "y2f": y2_far, "z": lambda ab: partner(),
        }
        for g in range(3):
            named[f"o{g}"] = functools.partial(lambda g, ab: x2_own(ab, g), g)
            named[f"pl{g}"] = functools.partial(lambda g, ab: x2_pass(ab, g, 1), g)
            named[f"pr{g}"] = functools.partial(lambda g, ab: x2_pass(ab, g, 2), g)
            named[f"l{g}"] = functools.partial(lambda g, ab: x2_last(ab, g), g)
        for d in range(8):
            named[f"m{d}"] = functools.partial(lambda d, ab: mul(ab, d), d)
        return named, last_rows, finish

    def run(p, sums, before_mul):
        named, last_rows, finish = steps(p)
        tail = len(PLAN)
        while PLAN[tail - 1][1][0] == "m":
            tail -= 1
        for ab, word in PLAN[:tail]:
            if word[0] == "m":
                before_mul()
            if ab < 2:
                named[word](ab)
            elif sums:
                sums[word]()
        places = [(ab, int(word[1])) for ab, word in PLAN[tail:]]
        for j in (3, 2, 1):
            part[p, j - 1] = last_rows(places, j).astype(jnp.bfloat16)
            push(part.at[p, j - 1], part_in.at[p, j - 1], rs_send.at[p], rs_recv.at[p], dev_rep(j))
        total = last_rows(places, 0)
        await_ref(part_in.at[p], rs_recv.at[p])
        for j in range(3):
            total = total + part_in[p, j].astype(jnp.float32)
        return total, finish

    pending = [fill] + loads[5:]

    def loaded():
        while pending:
            pending.pop().wait()

    total, finish0 = run(0, None, loaded)
    hidden = total.astype(jnp.bfloat16)
    pre_act = jnp.dot(hidden, weight[...], preferred_element_type=jnp.float32) + bias[...]
    gate = jax.nn.sigmoid(pre_act)
    pre_grad = (cotangent[...].astype(jnp.float32) * gate * (1.0 + pre_act * (1.0 - gate))).astype(jnp.bfloat16)
    store_own(1, lax.dot_general(
        pre_grad, weight[...], (((1,), (1,)), ((), ())), preferred_element_type=jnp.float32
    ).astype(jnp.bfloat16))
    acc[...] = jnp.zeros_like(acc)

    def terms():
        act_out[...] = (pre_act * gate).astype(jnp.bfloat16)
        weight_term = lax.dot_general(
            hidden, pre_grad, (((0,), (0,)), ((), ())), preferred_element_type=jnp.float32
        )
        bias_term = jnp.sum(pre_grad.astype(jnp.float32), axis=0, keepdims=True)
        rows = lax.broadcasted_iota(jnp.int32, (8, T), 0)
        bias_tile = jnp.where(rows == 0, bias_term[:, :T], jnp.where(rows == 1, bias_term[:, T:], 0.0))
        for piece in range(NZ):
            for t in range(4):
                wp[piece, t] = weight_term[piece * 16 + (t // 2) * 8:piece * 16 + (t // 2) * 8 + 8, (t % 2) * T:(t % 2) * T + T]
            wp[piece, 4] = bias_tile

    def ar1():
        terms()
        for j in (4, 3, 5, 2, 6, 1, 7):
            push(wp.at[(z + j) % NZ], wp_in.at[j - 1], ar_send.at[0], ar_recv.at[0], dev_z(j))

    def ar2():
        await_ref(wp_in, ar_recv.at[0])
        total = wp[z]
        for j in range(NZ - 1):
            total = total + wp_in[j]
        for t in range(4):
            w2[t, 0] = total[t]
            w2[t, 1] = total[4]
        for dx, dc, device in line_xc:
            push(w2.at[(x + dx) % NX], w2_in.at[((NX - dx) % NX) * 2 + dc - 1], ar_send.at[1], ar_recv.at[1], device)

    def ar3():
        await_ref(w2_in, ar_recv.at[1])
        total = w2[x]
        for j in range(7):
            total = total + w2_in[j]
        w3[...] = total
        for j, device in enumerate(line_y):
            push(w3, w3_in.at[j], ar_send.at[2], ar_recv.at[2], device)

    def ar4():
        await_ref(w3_in, ar_recv.at[2])
        total = w3[...]
        for j in range(NY - 1):
            total = total + w3_in[j]
        bgrad_out[:, :T] = total[1, 0:1]
        bgrad_out[:, T:] = total[1, 1:2]
        wq[x] = total[0]
        for dx in range(1, NX):
            push(wq.at[x], wq.at[x], ar_send.at[3], ar_recv.at[3], dev(dx=dx))

    def ar5():
        await_ref(wq.at[pl.ds(0, NX - 1)], ar_recv.at[3])
        wfull[z] = wq[...]
        for j in (4, 3, 5, 2, 6, 1, 7):
            push(wfull.at[z], wfull.at[z], ar_send.at[4], ar_recv.at[4], dev_z(j))

    total, finish1 = run(1, {"ar1": ar1, "ar2": ar2, "ar3": ar3, "ar4": ar4, "ar5": ar5}, lambda: None)
    grad = None
    for _ in range(3):
        piece = total.astype(jnp.bfloat16)
        total = total - piece.astype(jnp.float32)
        moved = jnp.dot(onehot, piece, preferred_element_type=jnp.float32)
        grad = moved if grad is None else grad + moved
    fgrad_out[...] = grad

    await_ref(wfull.at[pl.ds(0, NZ - 1)], ar_recv.at[4])
    for piece in range(8):
        for t in range(4):
            wgrad_out[pl.ds(piece * 16 + (t // 2) * 8, 8), pl.ds((t % 2) * T, T)] = wfull[piece, t]

    finish0()
    finish1()
    for p in range(2):
        await_ref(part.at[p], rs_send.at[p])
    await_ref(wp_in, ar_send.at[0])
    await_ref(w2_in, ar_send.at[1])
    await_ref(w3_in, ar_send.at[2])
    await_ref(wq.at[pl.ds(0, NX - 1)], ar_send.at[3])
    await_ref(wfull.at[pl.ds(0, NZ - 1)], ar_send.at[4])


def publish(*refs):
    sources, targets, staged, sems = refs[:4], refs[4:8], refs[8:12], refs[12]
    reads = [pltpu.make_async_copy(sources[i], staged[i], sems.at[0, i]) for i in range(4)]
    writes = [pltpu.make_async_copy(staged[i], targets[i], sems.at[1, i]) for i in range(4)]
    for copy in reads:
        copy.start()
    for read, write in zip(reads, writes):
        read.wait()
        write.start()
    for copy in writes:
        copy.wait()


def local(
    features, node_order, tile_values, tile_row, tile_col, tile_count, weight, bias_vec, cotangent
):
    vmem = pl.BlockSpec(memory_space=pltpu.VMEM)
    hbm = pl.BlockSpec(memory_space=pl.ANY)
    act, fgrad, wgrad, bgrad = pl.pallas_call(
        kernel,
        out_shape=(
            jax.ShapeDtypeStruct((T, 256), jnp.bfloat16),
            jax.ShapeDtypeStruct((T, T), jnp.float32),
            jax.ShapeDtypeStruct((T, 256), jnp.float32),
            jax.ShapeDtypeStruct((1, 256), jnp.float32),
        ),
        in_specs=[hbm] * 9,
        out_specs=(vmem, vmem, vmem, vmem),
        scratch_shapes=[
            pltpu.VMEM((T, T), jnp.bfloat16),
            pltpu.VMEM((1, T), jnp.int32),
            pltpu.VMEM((T, 256), jnp.bfloat16),
            pltpu.VMEM((1, 256), jnp.float32),
            pltpu.VMEM((T, 256), jnp.bfloat16),
            pltpu.SMEM((1, SLOTS), jnp.int32),
            pltpu.SMEM((1, SLOTS), jnp.int32),
            pltpu.SMEM((1, 1), jnp.int32),
            pltpu.VMEM((4, T), jnp.int32),
            pltpu.SMEM((4, T), jnp.int32),
            pltpu.VMEM((SLOTS + 1, T, T), jnp.bfloat16),
            pltpu.VMEM((2, 2, ROWS, T), jnp.bfloat16),
            pltpu.VMEM((4 * T, T), jnp.float32),
            pltpu.VMEM((2, 3, T, T), jnp.bfloat16),
            pltpu.VMEM((2, 3, T, T), jnp.bfloat16),
            pltpu.VMEM((8, 5, 8, T), jnp.float32),
            pltpu.VMEM((NZ - 1, 5, 8, T), jnp.float32),
            pltpu.VMEM((NX, 2, 8, T), jnp.float32),
            pltpu.VMEM((7, 2, 8, T), jnp.float32),
            pltpu.VMEM((2, 8, T), jnp.float32),
            pltpu.VMEM((NY - 1, 2, 8, T), jnp.float32),
            pltpu.VMEM((NX, 8, T), jnp.float32),
            pltpu.VMEM((NZ, 4, 8, T), jnp.float32),
            pltpu.SemaphoreType.DMA((9,)),
            pltpu.SemaphoreType.DMA,
            pltpu.SemaphoreType.DMA((2, N_RECV)),
            pltpu.SemaphoreType.DMA((2, 6)),
            pltpu.SemaphoreType.DMA((2,)),
            pltpu.SemaphoreType.DMA((2,)),
            pltpu.SemaphoreType.DMA((5,)),
            pltpu.SemaphoreType.DMA((5,)),
        ],
        compiler_params=pltpu.CompilerParams(
            collective_id=0, has_side_effects=True, vmem_limit_bytes=60 * 1024 * 1024
        ),
    )(
        features, node_order, tile_values.reshape(SLOTS, T, T), tile_row.reshape(1, SLOTS), tile_col.reshape(1, SLOTS),
        tile_count, weight, bias_vec.reshape(1, 256), cotangent,
    )
    anywhere = pl.BlockSpec(memory_space=pl.ANY)
    act, fgrad, wgrad, bgrad = pl.pallas_call(
        publish,
        out_shape=tuple(jax.ShapeDtypeStruct(a.shape, a.dtype) for a in (act, fgrad, wgrad, bgrad)),
        in_specs=[anywhere] * 4,
        out_specs=(anywhere,) * 4,
        scratch_shapes=[pltpu.VMEM(a.shape, a.dtype) for a in (act, fgrad, wgrad, bgrad)] + [pltpu.SemaphoreType.DMA((2, 4))],
        compiler_params=pltpu.CompilerParams(vmem_limit_bytes=60 * 1024 * 1024),
    )(act, fgrad, wgrad, bgrad)
    return act, fgrad, wgrad, bgrad.reshape(256)


def solution(mesh):
    return jax.shard_map(
        local,
        mesh=mesh,
        in_specs=(
            P(("rep", "row"), None),
            P(("rep", "row"), None),
            P("rep", "row", None, None, None),
            P("rep", "row", None),
            P("rep", "row", None),
            P("rep", "row"),
            P(),
            P(),
            P(("rep", "row"), None),
        ),
        out_specs=(P(("rep", "row"), None), P(("rep", "row"), None), P(), P()),
        check_vma=False,
    )
```

```python
import functools

import jax
import jax.numpy as jnp
from jax import lax
from jax.experimental import pallas as pl
from jax.experimental.pallas import tpu as pltpu
from jax.sharding import PartitionSpec as P

MESH = pl.DeviceIdType.MESH
NX, NY, NZ = 4, 8, 8
T = 128
R1, R2 = 32, 96
SLOTS = 135
GROUPS = ((0, 1), (1, 4), (5, 3))
GROUP_OF = (0, 1, 1, 1, 1, 2, 2, 2)
DIRECT = ()
ROWS = 64 * (R1 + R2)


def row1(ab, d, xi):
    return ((ab * 8 + d) * 4 + xi) * R1


def row2(ab, xi, d):
    return 64 * R1 + ((ab * 4 + xi) * 8 + d) * R2


PLAN = (
    (0, "z"), (0, "y2s"), (0, "x1s"), (2, "ar1"), (0, "y1n1"), (0, "o0"), (0, "y2f"), (0, "o1"), (1, "x1s"),
    (1, "y2s"), (0, "pl0"), (1, "o0"), (0, "pr0"), (0, "y1n2"), (2, "ar2"), (0, "o2"), (0, "pl1"), (0, "pr1"),
    (1, "y2f"), (1, "pr0"), (1, "o1"), (1, "y1n2"), (0, "l0"), (2, "ar3"), (0, "m0"), (0, "y1f"), (0, "pr2"),
    (1, "pl0"), (1, "y1n1"), (0, "pl2"), (0, "y1b"), (0, "l1"), (1, "o2"), (1, "l0"), (0, "m2"), (0, "m3"),
    (1, "pl1"), (1, "pr1"), (1, "y1f"), (0, "m4"), (1, "m0"), (0, "l2"), (0, "y1l"), (2, "ar4"), (1, "pr2"),
    (0, "m1"), (1, "pl2"), (1, "y1b"), (0, "m7"), (1, "l1"), (0, "m5"), (0, "m6"), (1, "y1l"), (1, "m2"), (1, "m3"),
    (1, "l2"), (2, "ar5"), (1, "m4"), (1, "m1"), (1, "m5"), (1, "m6"), (1, "m7"),
)


SEM_Z = 0


def sem_x1(ab):
    return 1 + ab


def sem_y1(ab, step):
    return 3 + ab * 3 + step


def sem_y2(ab, step):
    return 9 + ab * 2 + step


def sem_x2(ab, xi, g):
    return 13 + (ab * 3 + xi - 1) * 3 + g


def sem_sib(ab, g):
    return 31 + ab * 3 + g


N_RECV = 37
SEND_Z, SEND_X1, SEND_Y1, SEND_Y2, SEND_X2, SEND_SIB = range(6)


def kernel(
    features_hbm, order_hbm, tiles_hbm, row_hbm, col_hbm, count_hbm, weight_hbm, bias_hbm, cotangent_hbm,
    act_out, fgrad_out, wgrad_out, bgrad_out,
    features, order, weight, bias, cotangent, tile_row, tile_col, tile_count, found, table,
    tiles, G, acc, part, part_in, wp, wp_in, w2, w2_in, w3, w3_in, wq, wfull,
    load_sem, fill_sem, recv, send, rs_recv, rs_send, ar_recv, ar_send,
):
    q = lax.axis_index("rep")
    r = lax.axis_index("row")
    y, zh, x, c = r // 16, (r // 8) % 2, (r // 2) % 4, r % 2
    z = zh * 4 + q

    def dev(dy=0, dx=0, dc=0):
        ny, nx, nc = (y + dy) % NY, (x + dx) % NX, (c + dc) % 2
        return (q, ny * 16 + zh * 8 + nx * 2 + nc)

    def dev_z(dz):
        nz = (z + dz) % NZ
        return (nz % 4, y * 16 + (nz // 4) * 8 + x * 2 + c)

    def dev_rep(dq):
        return ((q + dq) % 4, r)

    z_partner = dev_z(4)
    along_y = {j: dev(dy=j % NY) for j in (-2, -1, 1, 2)}
    along_x = {j: dev(dx=j % NX) for j in (-1, 1, 2)}
    sibling = dev(dc=1)
    line_y = [dev(dy=j) for j in range(1, NY)]
    line_xc = [(dx, dc, dev(dx=dx, dc=dc)) for dx in range(NX) for dc in range(2) if dx or dc]
    line_z = [dev_z(j) for j in range(1, NZ)]

    barrier = pltpu.get_barrier_semaphore()
    for peer in line_y + [p for _, _, p in line_xc] + line_z:
        pl.semaphore_signal(barrier, inc=1, device_id=peer, device_id_type=MESH)

    loads = [
        pltpu.make_async_copy(src, dst, load_sem.at[i]) for i, (src, dst) in enumerate((
            (row_hbm, tile_row), (col_hbm, tile_col), (count_hbm, tile_count), (features_hbm, features), (order_hbm, order),
            (tiles_hbm, tiles.at[pl.ds(0, SLOTS)]), (weight_hbm, weight), (bias_hbm, bias), (cotangent_hbm, cotangent),
        ))
    ]
    for load in loads:
        load.start()
    tiles[SLOTS] = jnp.zeros((T, T), jnp.bfloat16)

    acc[...] = jnp.zeros_like(acc)
    for load in loads[:5]:
        load.wait()
    places = lax.broadcasted_iota(jnp.int32, (T, T), 0) == order[...]
    onehot = places.astype(jnp.float32).astype(jnp.bfloat16)

    def store_own(p, block):
        G[p, 0, pl.ds(row1(0, 0, 0), R1)] = block[:R1]
        G[p, 0, pl.ds(row2(0, 0, 0), R2)] = block[R1:]

    store_own(0, lax.dot_general(
        onehot, features[...], (((0,), (0,)), ((), ())), preferred_element_type=jnp.float32
    ).astype(jnp.bfloat16))

    place = lax.broadcasted_iota(jnp.int32, (4, T), 0) * T + lax.broadcasted_iota(jnp.int32, (4, T), 1)
    j, k, xi, d, ab = place & 3, (place >> 2) & 1, (place >> 3) & 3, (place >> 5) & 7, place >> 8
    dy = jnp.where(d == 7, 4, jnp.where((d & 1) == 1, -((d + 1) >> 1), d >> 1))
    dx = jnp.where(xi == 3, 2, jnp.where(xi == 1, -1, xi >> 1))
    column = ((y + dy) & 7) * 16 + ((zh + ab) & 1) * 8 + ((x + dx) & 3) * 2 + ((c + k) & 1)
    want = column * 4 + ((q + j) & 3)
    used = tile_count[0, 0]

    def look(slot, at):
        key = jnp.where(slot < used, tile_col[0, slot] * 4 + tile_row[0, slot], -1)
        return jnp.where(want == key, slot, at)

    found[...] = lax.fori_loop(0, SLOTS, look, jnp.full((4, T), SLOTS, jnp.int32), unroll=5)
    fill = pltpu.make_async_copy(found, table, fill_sem)
    fill.start()

    pl.semaphore_wait(barrier, 21)

    def push(src, dst, send_sem, recv_sem, device):
        pltpu.make_async_remote_copy(
            src_ref=src, dst_ref=dst, send_sem=send_sem, recv_sem=recv_sem,
            device_id=device, device_id_type=MESH,
        ).start()

    def await_ref(ref, sem):
        pltpu.make_async_copy(ref, ref, sem).wait()

    def steps(p):
        own = G.at[p, 0]
        other = G.at[p, 1]
        waited = set()

        def go(src, dst, n, kind, sem, device):
            push(own.at[pl.ds(src, n)], own.at[pl.ds(dst, n)], send.at[p, kind], recv.at[p, sem], device)

        def ensure(sem, n):
            if sem not in waited:
                waited.add(sem)
                await_ref(own.at[pl.ds(0, n)], recv.at[p, sem])

        def sib(at, n, ab, g):
            push(own.at[pl.ds(at, n)], other.at[pl.ds(at, n)], send.at[p, SEND_SIB], recv.at[p, sem_sib(ab, g)], sibling)

        def sib1(ab, d, n, g):
            sib(row1(ab, d, 0), n * 4 * R1, ab, g)

        def sib2(ab, xi, g):
            sib(row2(ab, xi, GROUPS[g][0]), GROUPS[g][1] * R2, ab, g)

        def y1(ab, src, dst, step, dy):
            go(row1(ab, src, 0), row1(ab, dst, 0), 4 * R1, SEND_Y1, sem_y1(ab, step), along_y[dy])

        def y2(ab, src, dst, step, dy):
            go(row2(ab, 0, src), row2(ab, 0, dst), R2, SEND_Y2, sem_y2(ab, step), along_y[dy])

        def x2(ab, src, dst, g, dx, first=0, n=None):
            d, n = GROUPS[g][0] + first, GROUPS[g][1] if n is None else n
            if n:
                go(row2(ab, src, d), row2(ab, dst, d), n * R2, SEND_X2, sem_x2(ab, dst, g), along_x[dx])

        def own_ready(ab):
            if ab == 1:
                ensure(SEM_Z, R1 + R2)

        def partner():
            go(row1(0, 0, 0), row1(1, 0, 0), R1, SEND_Z, SEM_Z, z_partner)
            go(row2(0, 0, 0), row2(1, 0, 0), R2, SEND_Z, SEM_Z, z_partner)

        def y2_start(ab):
            own_ready(ab)
            for dst, dy in ((3, 2), (4, -2), (1, 1), (2, -1)):
                y2(ab, 0, dst, 0, dy)

        def x1_start(ab):
            own_ready(ab)
            for dx, xi in ((2, 3), (1, 1), (-1, 2)):
                go(row1(ab, 0, 0), row1(ab, 0, xi), R1, SEND_X1, sem_x1(ab), along_x[dx])

        def x2_own(ab, g):
            if g == 0:
                own_ready(ab)
            else:
                ensure(sem_y2(ab, g - 1), (4, 3)[g - 1] * R2)
            if (ab, g) in DIRECT:
                x2(ab, 0, 3, g, 2)
            x2(ab, 0, 1, g, 1)
            x2(ab, 0, 2, g, -1)
            sib2(ab, 0, g)

        def x2_pass(ab, g, xi):
            n = GROUPS[g][1]
            half = (n + 1 - ab) // 2
            ensure(sem_x2(ab, xi, g), n * R2)
            if (ab, g) not in DIRECT:
                if xi == 1:
                    x2(ab, 1, 3, g, 1, 0, half)
                else:
                    x2(ab, 2, 3, g, -1, half, n - half)
            sib2(ab, xi, g)

        def x2_last(ab, g):
            ensure(sem_x2(ab, 3, g), GROUPS[g][1] * R2)
            sib2(ab, 3, g)

        def y1_two(ab):
            ensure(sem_x1(ab), 3 * R1)
            y1(ab, 0, 3, 1, 2)
            y1(ab, 0, 4, 1, -2)

        def y1_one(ab):
            ensure(sem_x1(ab), 3 * R1)
            y1(ab, 0, 1, 0, 1)
            y1(ab, 0, 2, 0, -1)
            sib1(ab, 0, 1, 0)

        def y1_near(ab):
            ensure(sem_y1(ab, 0), 8 * R1)
            sib1(ab, 1, 2, 1)

        def y1_far(ab):
            ensure(sem_y1(ab, 1), 8 * R1)
            if ab == 0:
                y1(ab, 3, 7, 2, 2)
            else:
                y1(ab, 4, 7, 2, -2)
            y1(ab, 3, 5, 2, 1)
            y1(ab, 4, 6, 2, -1)
            sib1(ab, 3, 2, 1)

        def y1_last(ab):
            ensure(sem_y1(ab, 2), 12 * R1)
            sib1(ab, 5, 3, 2)

        def y2_far(ab):
            ensure(sem_y2(ab, 0), 4 * R2)
            if ab == 0:
                y2(ab, 3, 7, 1, 2)
            else:
                y2(ab, 4, 7, 1, -2)
            y2(ab, 3, 5, 1, 1)
            y2(ab, 4, 6, 1, -1)

        def columns(ab, d):
            pieces = []
            for xi in range(4):
                for k in range(2):
                    pieces.append(G[p, k, pl.ds(row1(ab, d, xi), R1)])
                    pieces.append(G[p, k, pl.ds(row2(ab, xi, d), R2)])
            return pieces

        def blocks(ab, d, j):
            base = (ab * 8 + d) * 32 + j
            return [tiles[table[(base + col * 4) // T, (base + col * 4) % T]] for col in range(8)]

        def arrived(ab, d):
            g = GROUP_OF[d]
            ensure(sem_sib(ab, g), GROUPS[g][1] * 512)

        def mul(ab, d):
            arrived(ab, d)
            left = jnp.concatenate([jnp.concatenate(blocks(ab, d, j), axis=1) for j in range(4)], axis=0)
            acc[...] += jnp.dot(left, jnp.concatenate(columns(ab, d), axis=0), preferred_element_type=jnp.float32)

        def last_rows(places, j):
            total = acc[pl.ds(j * T, T)]
            for ab, d in places:
                arrived(ab, d)
                total = total + jnp.dot(
                    jnp.concatenate(blocks(ab, d, j), axis=1), jnp.concatenate(columns(ab, d), axis=0),
                    preferred_element_type=jnp.float32,
                )
            return total

        def finish():
            for kind, n in ((SEND_Z, R1 + R2), (SEND_X1, 6 * R1), (SEND_Y1, 56 * R1), (SEND_Y2, 14 * R2), (SEND_X2, 48 * R2), (SEND_SIB, ROWS)):
                await_ref(own.at[pl.ds(0, n)], send.at[p, kind])

        named = {
            "y2s": y2_start, "x1s": x1_start, "y1n2": y1_two, "y1n1": y1_one, "y1b": y1_near, "y1f": y1_far,
            "y1l": y1_last, "y2f": y2_far, "z": lambda ab: partner(),
        }
        for g in range(3):
            named[f"o{g}"] = functools.partial(lambda g, ab: x2_own(ab, g), g)
            named[f"pl{g}"] = functools.partial(lambda g, ab: x2_pass(ab, g, 1), g)
            named[f"pr{g}"] = functools.partial(lambda g, ab: x2_pass(ab, g, 2), g)
            named[f"l{g}"] = functools.partial(lambda g, ab: x2_last(ab, g), g)
        for d in range(8):
            named[f"m{d}"] = functools.partial(lambda d, ab: mul(ab, d), d)
        return named, last_rows, finish

    def run(p, sums, before_mul):
        named, last_rows, finish = steps(p)
        tail = len(PLAN)
        while PLAN[tail - 1][1][0] == "m":
            tail -= 1
        for ab, word in PLAN[:tail]:
            if word[0] == "m":
                before_mul()
            if ab < 2:
                named[word](ab)
            elif sums:
                sums[word]()
        places = [(ab, int(word[1])) for ab, word in PLAN[tail:]]
        for j in (3, 2, 1):
            part[p, j - 1] = last_rows(places, j).astype(jnp.bfloat16)
            push(part.at[p, j - 1], part_in.at[p, j - 1], rs_send.at[p], rs_recv.at[p], dev_rep(j))
        total = last_rows(places, 0)
        await_ref(part_in.at[p], rs_recv.at[p])
        for j in range(3):
            total = total + part_in[p, j].astype(jnp.float32)
        return total, finish

    pending = [fill] + loads[5:]

    def loaded():
        while pending:
            pending.pop().wait()

    total, finish0 = run(0, None, loaded)
    hidden = total.astype(jnp.bfloat16)
    pre_act = jnp.dot(hidden, weight[...], preferred_element_type=jnp.float32) + bias[...]
    gate = jax.nn.sigmoid(pre_act)
    pre_grad = (cotangent[...].astype(jnp.float32) * gate * (1.0 + pre_act * (1.0 - gate))).astype(jnp.bfloat16)
    store_own(1, lax.dot_general(
        pre_grad, weight[...], (((1,), (1,)), ((), ())), preferred_element_type=jnp.float32
    ).astype(jnp.bfloat16))
    acc[...] = jnp.zeros_like(acc)

    def terms():
        act_out[...] = (pre_act * gate).astype(jnp.bfloat16)
        weight_term = lax.dot_general(
            hidden, pre_grad, (((0,), (0,)), ((), ())), preferred_element_type=jnp.float32
        )
        bias_term = jnp.sum(pre_grad.astype(jnp.float32), axis=0, keepdims=True)
        rows = lax.broadcasted_iota(jnp.int32, (8, T), 0)
        bias_tile = jnp.where(rows == 0, bias_term[:, :T], jnp.where(rows == 1, bias_term[:, T:], 0.0))
        for piece in range(NZ):
            for t in range(4):
                wp[piece, t] = weight_term[piece * 16 + (t // 2) * 8:piece * 16 + (t // 2) * 8 + 8, (t % 2) * T:(t % 2) * T + T]
            wp[piece, 4] = bias_tile

    def ar1():
        terms()
        for j in (4, 3, 5, 2, 6, 1, 7):
            push(wp.at[(z + j) % NZ], wp_in.at[j - 1], ar_send.at[0], ar_recv.at[0], dev_z(j))

    def ar2():
        await_ref(wp_in, ar_recv.at[0])
        total = wp[z]
        for j in range(NZ - 1):
            total = total + wp_in[j]
        for t in range(4):
            w2[t, 0] = total[t]
            w2[t, 1] = total[4]
        for dx, dc, device in line_xc:
            push(w2.at[(x + dx) % NX], w2_in.at[((NX - dx) % NX) * 2 + dc - 1], ar_send.at[1], ar_recv.at[1], device)

    def ar3():
        await_ref(w2_in, ar_recv.at[1])
        total = w2[x]
        for j in range(7):
            total = total + w2_in[j]
        w3[...] = total
        for j, device in enumerate(line_y):
            push(w3, w3_in.at[j], ar_send.at[2], ar_recv.at[2], device)

    def ar4():
        await_ref(w3_in, ar_recv.at[2])
        total = w3[...]
        for j in range(NY - 1):
            total = total + w3_in[j]
        bgrad_out[:, :T] = total[1, 0:1]
        bgrad_out[:, T:] = total[1, 1:2]
        wq[x] = total[0]
        for dx in range(1, NX):
            push(wq.at[x], wq.at[x], ar_send.at[3], ar_recv.at[3], dev(dx=dx))

    def ar5():
        await_ref(wq.at[pl.ds(0, NX - 1)], ar_recv.at[3])
        wfull[z] = wq[...]
        for j in (4, 3, 5, 2, 6, 1, 7):
            push(wfull.at[z], wfull.at[z], ar_send.at[4], ar_recv.at[4], dev_z(j))

    total, finish1 = run(1, {"ar1": ar1, "ar2": ar2, "ar3": ar3, "ar4": ar4, "ar5": ar5}, lambda: None)
    grad = None
    for _ in range(3):
        piece = total.astype(jnp.bfloat16)
        total = total - piece.astype(jnp.float32)
        moved = jnp.dot(onehot, piece, preferred_element_type=jnp.float32)
        grad = moved if grad is None else grad + moved
    fgrad_out[...] = grad

    await_ref(wfull.at[pl.ds(0, NZ - 1)], ar_recv.at[4])
    for piece in range(8):
        for t in range(4):
            wgrad_out[pl.ds(piece * 16 + (t // 2) * 8, 8), pl.ds((t % 2) * T, T)] = wfull[piece, t]

    finish0()
    finish1()
    for p in range(2):
        await_ref(part.at[p], rs_send.at[p])
    await_ref(wp_in, ar_send.at[0])
    await_ref(w2_in, ar_send.at[1])
    await_ref(w3_in, ar_send.at[2])
    await_ref(wq.at[pl.ds(0, NX - 1)], ar_send.at[3])
    await_ref(wfull.at[pl.ds(0, NZ - 1)], ar_send.at[4])


def publish(*refs):
    sources, targets, staged, sems = refs[:4], refs[4:8], refs[8:12], refs[12]
    reads = [pltpu.make_async_copy(sources[i], staged[i], sems.at[0, i]) for i in range(4)]
    writes = [pltpu.make_async_copy(staged[i], targets[i], sems.at[1, i]) for i in range(4)]
    for copy in reads:
        copy.start()
    for read, write in zip(reads, writes):
        read.wait()
        write.start()
    for copy in writes:
        copy.wait()


def local(
    features, node_order, tile_values, tile_row, tile_col, tile_count, weight, bias_vec, cotangent
):
    vmem = pl.BlockSpec(memory_space=pltpu.VMEM)
    hbm = pl.BlockSpec(memory_space=pl.ANY)
    act, fgrad, wgrad, bgrad = pl.pallas_call(
        kernel,
        out_shape=(
            jax.ShapeDtypeStruct((T, 256), jnp.bfloat16),
            jax.ShapeDtypeStruct((T, T), jnp.float32),
            jax.ShapeDtypeStruct((T, 256), jnp.float32),
            jax.ShapeDtypeStruct((1, 256), jnp.float32),
        ),
        in_specs=[hbm] * 9,
        out_specs=(vmem, vmem, vmem, vmem),
        scratch_shapes=[
            pltpu.VMEM((T, T), jnp.bfloat16),
            pltpu.VMEM((1, T), jnp.int32),
            pltpu.VMEM((T, 256), jnp.bfloat16),
            pltpu.VMEM((1, 256), jnp.float32),
            pltpu.VMEM((T, 256), jnp.bfloat16),
            pltpu.SMEM((1, SLOTS), jnp.int32),
            pltpu.SMEM((1, SLOTS), jnp.int32),
            pltpu.SMEM((1, 1), jnp.int32),
            pltpu.VMEM((4, T), jnp.int32),
            pltpu.SMEM((4, T), jnp.int32),
            pltpu.VMEM((SLOTS + 1, T, T), jnp.bfloat16),
            pltpu.VMEM((2, 2, ROWS, T), jnp.bfloat16),
            pltpu.VMEM((4 * T, T), jnp.float32),
            pltpu.VMEM((2, 3, T, T), jnp.bfloat16),
            pltpu.VMEM((2, 3, T, T), jnp.bfloat16),
            pltpu.VMEM((8, 5, 8, T), jnp.float32),
            pltpu.VMEM((NZ - 1, 5, 8, T), jnp.float32),
            pltpu.VMEM((NX, 2, 8, T), jnp.float32),
            pltpu.VMEM((7, 2, 8, T), jnp.float32),
            pltpu.VMEM((2, 8, T), jnp.float32),
            pltpu.VMEM((NY - 1, 2, 8, T), jnp.float32),
            pltpu.VMEM((NX, 8, T), jnp.float32),
            pltpu.VMEM((NZ, 4, 8, T), jnp.float32),
            pltpu.SemaphoreType.DMA((9,)),
            pltpu.SemaphoreType.DMA,
            pltpu.SemaphoreType.DMA((2, N_RECV)),
            pltpu.SemaphoreType.DMA((2, 6)),
            pltpu.SemaphoreType.DMA((2,)),
            pltpu.SemaphoreType.DMA((2,)),
            pltpu.SemaphoreType.DMA((5,)),
            pltpu.SemaphoreType.DMA((5,)),
        ],
        compiler_params=pltpu.CompilerParams(
            collective_id=0, has_side_effects=True, vmem_limit_bytes=60 * 1024 * 1024
        ),
    )(
        features, node_order, tile_values.reshape(SLOTS, T, T), tile_row.reshape(1, SLOTS), tile_col.reshape(1, SLOTS),
        tile_count, weight, bias_vec.reshape(1, 256), cotangent,
    )
    anywhere = pl.BlockSpec(memory_space=pl.ANY)
    act, fgrad, wgrad, bgrad = pl.pallas_call(
        publish,
        out_shape=tuple(jax.ShapeDtypeStruct(a.shape, a.dtype) for a in (act, fgrad, wgrad, bgrad)),
        in_specs=[anywhere] * 4,
        out_specs=(anywhere,) * 4,
        scratch_shapes=[pltpu.VMEM(a.shape, a.dtype) for a in (act, fgrad, wgrad, bgrad)] + [pltpu.SemaphoreType.DMA((2, 4))],
        compiler_params=pltpu.CompilerParams(vmem_limit_bytes=60 * 1024 * 1024),
    )(act, fgrad, wgrad, bgrad)
    return act, fgrad, wgrad, bgrad.reshape(256)


def solution(mesh):
    return jax.shard_map(
        local,
        mesh=mesh,
        in_specs=(
            P(("rep", "row"), None),
            P(("rep", "row"), None),
            P("rep", "row", None, None, None),
            P("rep", "row", None),
            P("rep", "row", None),
            P("rep", "row"),
            P(),
            P(),
            P(("rep", "row"), None),
        ),
        out_specs=(P(("rep", "row"), None), P(("rep", "row"), None), P(), P()),
        check_vma=False,
    )
```
